32 devices in a mesh: leaf: 2 (over x), blk: 4 (over y, core), kv: 4 (over z).
Axes of the slice: x: 2, y: 2, z: 4, core: 2. Of those that a mesh axis runs over, the one named last changes fastest.
Arguments:
- queries: bfloat16 [4096, 2560], P(('leaf', 'blk', 'kv')), parts along dimension 0, may hold values from -8 to 8
- keys: bfloat16 [16384, 512], P(('leaf', 'blk', 'kv')), parts along dimension 0, may hold values from -8 to 8
- values: bfloat16 [16384, 512], P(('leaf', 'blk', 'kv')), parts along dimension 0, may hold values from -6 to 6
- ancestry: int32 [32, 64], P('leaf'), parts along dimension 0, may hold values from 0 to 1, as said below
- leaf_tiles: int32 [32], P('leaf'), parts along dimension 0, may hold values from 1 to 63, as said below
Outputs:
- attended: bfloat16 [4096, 2560], P(('leaf', 'blk', 'kv')), parts along dimension 0
The draws below stay inside these ranges and needn't reach their ends.
There are 2 independent parts, one for each index of `leaf`. The reference program is written for one: setup_inputs(seed, part) draws one part's arguments, and reference() takes and returns one part's arrays. A program takes and returns all parts, laid end to end along the dimension named above; each array names one. Nothing has to cross between parts.
Inputs may be any that keep to these rules, and one draw needn't show every extreme that they name: ancestry[a, t] is 1 exactly when key tile t is a strict ancestor of tile leaf_tiles[a] in the tree whose nodes are the key tiles; tile 0 is the root of the tree. `leaf_tiles`: strictly rising; the last entry is 63.
All inputs are finite; a program needn't handle non-finite values.
Results may differ from the reference program's by a relative error of at most 0.018.
Values may be sent and summed in bfloat16 or wider, within the bound.
A program may use at most 256 MiB of HBM per device.

```python
import jax
import jax.numpy as jnp
from jax import lax

TILE = 128
KV_HEADS = 4
GROUP = 5
DH = 128
QUERIES = 2048
KEYS = 8192
Q_TILES = 16
K_TILES = 64


def tree_shape(key):
    tile_count = K_TILES
    leaf_count = Q_TILES
    window = max(1, K_TILES // 4)
    parent_key = jax.random.fold_in(key, 11)
    leaf_key = jax.random.fold_in(key, 12)
    tile_ids = jnp.arange(tile_count, dtype=jnp.int32)
    lowest = jnp.maximum(tile_ids - window, 0)
    spread = jax.random.randint(parent_key, (tile_count,), 0, 1 << 20, dtype=jnp.int32)
    parent = jnp.where(tile_ids > 0, lowest + spread % jnp.maximum(tile_ids - lowest, 1), 0).astype(jnp.int32)
    shuffled = jax.random.permutation(leaf_key, tile_count - 2).astype(jnp.int32) + 1
    chosen = jnp.sort(shuffled[:leaf_count - 1])
    leaves = jnp.concatenate([chosen, jnp.full((1,), tile_count - 1, jnp.int32)]).astype(jnp.int32)

    def climb_up(index_, carried):
        ancestors, current = carried
        current = parent[current]
        ancestors = jnp.maximum(ancestors, (tile_ids[None, :] == current[:, None]).astype(jnp.int32))
        return (ancestors, current)
    ancestors, _ = lax.fori_loop(0, tile_count, climb_up, (jnp.zeros((leaf_count, tile_count), jnp.int32), leaves))
    return (ancestors, leaves)


def draw_ancestry(key, part):
    ancestors, leaves = tree_shape(key)
    return ancestors


def draw_leaf_tiles(key, part):
    ancestors, leaves = tree_shape(key)
    return leaves


def draw_queries(key, part):
    key = jax.random.fold_in(key, 3)
    shape_all = (QUERIES, KV_HEADS * GROUP * DH)
    result = jax.random.truncated_normal(key, -6.0, 6.0, shape_all, jnp.float32)
    return result.astype(jnp.bfloat16)


def draw_keys(key, part):
    key = jax.random.fold_in(key, 4)
    shape_all = (KEYS, KV_HEADS * DH)
    result = jax.random.truncated_normal(key, -6.0, 6.0, shape_all, jnp.float32)
    return result.astype(jnp.bfloat16)


def level_of(key, shape, pieces, low, high):
    def one(dim, shards_of):
        draws = jax.random.uniform(jax.random.fold_in(jax.random.fold_in(key, 6), dim), (shards_of,), jnp.float32, low / len(pieces), high / len(pieces))
        return jnp.repeat(jnp.exp(draws), shape[dim] // shards_of).reshape((-1,) + (1,) * (len(shape) - dim - 1))

    factor_of = one(*pieces[0])
    for cut in pieces[1:]:
        factor_of = factor_of * one(*cut)
    return factor_of


def normal_values(rng, extent, deviation, reach, pieces=(), kind=jnp.bfloat16):
    loudness = level_of(rng, extent, pieces, -0.22, 0.18) if pieces else 1.0
    drawn = jax.random.normal(rng, extent, jnp.float32) * deviation * loudness
    return jnp.minimum(jnp.maximum(drawn, -reach), reach).astype(kind)


def setup_inputs(seed: int = 0, part: int = 0) -> dict:
    key_list = jax.random.split(jax.random.key(seed), 6)
    part_splits = jax.random.split(jax.random.fold_in(key_list[5], part), 6)
    return {
        "queries": draw_queries(jax.random.fold_in(jax.random.fold_in(key_list[5], part), 71), part),
        "keys": draw_keys(jax.random.fold_in(jax.random.fold_in(key_list[5], part), 71), part),
        "values": normal_values(part_splits[2], (KEYS, KV_HEADS * DH), 1.0, 6.0, ((0, 16),)),
        "ancestry": draw_ancestry(jax.random.fold_in(jax.random.fold_in(key_list[5], part), 71), part),
        "leaf_tiles": draw_leaf_tiles(jax.random.fold_in(jax.random.fold_in(key_list[5], part), 71), part),
    }


def reference(queries, keys, values, ancestry, leaf_tiles):
    query_ids = jnp.arange(QUERIES, dtype=jnp.int32)
    key_ids = jnp.arange(KEYS, dtype=jnp.int32)
    query_tiles = query_ids // TILE
    key_tiles = key_ids // TILE
    own_tile = leaf_tiles[query_tiles]
    linked = ancestry[query_tiles][:, key_tiles] == 1
    causal = (key_ids % TILE)[None, :] <= (query_ids % TILE)[:, None]
    allowed = jnp.where(key_tiles[None, :] == own_tile[:, None], causal, linked)
    query_heads = queries.reshape(QUERIES, KV_HEADS, GROUP, DH)
    key_heads = keys.reshape(KEYS, KV_HEADS, DH)
    value_heads = values.reshape(KEYS, KV_HEADS, DH)
    scaling = 1.0 / jnp.sqrt(jnp.float32(DH))

    def one_head(head_id):
        query_part = query_heads[:, head_id].astype(jnp.float32)
        key_part = key_heads[:, head_id].astype(jnp.float32)
        value_part = value_heads[:, head_id].astype(jnp.float32)
        scores = jnp.einsum('qgd,sd->gqs', query_part, key_part) * scaling
        scores = jnp.where(allowed[None], scores, -1e+30)
        row_peak = lax.optimization_barrier(jnp.max(scores, axis=-1))
        weights = jnp.where(allowed[None], jnp.exp(scores - row_peak[..., None]), 0.0)
        row_total = lax.optimization_barrier(jnp.sum(weights, axis=-1))
        rounded = lax.optimization_barrier(weights.astype(jnp.bfloat16)).astype(jnp.float32)
        summed = jnp.einsum('gqs,sd->qgd', rounded, value_part)
        return summed / jnp.transpose(row_total, (1, 0))[..., None]
    result = lax.map(one_head, jnp.arange(KV_HEADS, dtype=jnp.int32))
    result = jnp.transpose(result, (1, 0, 2, 3)).reshape(QUERIES, KV_HEADS * GROUP * DH)
    return result.astype(jnp.bfloat16)
```

```python
import functools
import math

import jax
import jax.numpy as jnp
from jax import lax
from jax.experimental import pallas as pl
from jax.experimental.pallas import tpu as pltpu
from jax.sharding import PartitionSpec as P

TILE = 128
KV_HEADS = 4
GROUP = 5
DH = 128
WIDE = GROUP * DH
MESH = pl.DeviceIdType.MESH
NEG = -1e30
EXP2_SCALE = math.log2(math.e) / math.sqrt(DH)

KV_OFFSETS = ((0, 3), (1, 3), (0, 2), (1, 2), (1, 1), (0, 1), (1, 0))
GROUP_OFFSETS = ((1, 1), (0, 1), (1, 0))


class Place:
    def __init__(self):
        self.leaf = lax.axis_index("leaf")
        self.blk = lax.axis_index("blk")
        self.z = lax.axis_index("kv")
        self.y = self.blk // 2
        self.core = self.blk % 2

    def partner(self, dy, dz):
        y = 1 - self.y if dy else self.y
        z = self.z
        if dz == 1:
            z = z + 1 - 2 * (z % 2)
        elif dz == 2:
            z = (z + 2) % 4
        elif dz == 3:
            z = 3 - z
        return y, z

    def device(self, y, core, z):
        return (self.leaf, 2 * y + core, z)


def head_of(y, z):
    return 2 * y + z % 2


def aligned(index, size):
    return pl.ds(pl.multiple_of(index * size, size), size)


def greet(devices):
    barrier = pltpu.get_barrier_semaphore()
    for device in devices:
        pl.semaphore_signal(barrier, inc=1, device_id=device, device_id_type=MESH)
    pl.semaphore_wait(barrier, len(devices))


def gather_kernel(
    q_ref, k_ref, v_ref, q_all, k_all, v_all,
    kv_send, kv_recv, pass_send, pass_recv, q_send, q_recv, own_sem,
):
    at = Place()
    rows = k_ref.shape[0]
    sibling = at.device(at.y, 1 - at.core, at.z)
    partners = [at.partner(dy, dz) for dy, dz in KV_OFFSETS]
    greet([at.device(y, at.core, z) for y, z in partners] + [sibling])

    head = head_of(at.y, at.z)
    here = aligned(at.blk * 4 + at.z, rows)

    def rows_of(y, core, z):
        return aligned((2 * y + core) * 4 + z, rows)

    kv = ((k_ref, k_all), (v_ref, v_all))

    def send_kv(i):
        y, z = partners[i]
        copies = []
        for w, (own, whole) in enumerate(kv):
            copies.append(
                pltpu.make_async_remote_copy(
                    src_ref=own.at[:, aligned(head_of(y, z), DH)],
                    dst_ref=whole.at[here],
                    send_sem=kv_send.at[2 * i + w],
                    recv_sem=kv_recv.at[2 * i + w],
                    device_id=at.device(y, at.core, z),
                    device_id_type=MESH,
                )
            )
        return copies

    def arrive_kv(i):
        y, z = partners[i]
        return [
            pltpu.make_async_remote_copy(
                src_ref=own.at[:, aligned(head, DH)],
                dst_ref=whole.at[rows_of(y, at.core, z)],
                send_sem=kv_send.at[2 * i + w],
                recv_sem=kv_recv.at[2 * i + w],
                device_id=at.device(y, at.core, z),
                device_id_type=MESH,
            )
            for w, (own, whole) in enumerate(kv)
        ]

    def send_q(i):
        y, z = at.partner(*GROUP_OFFSETS[i])
        return pltpu.make_async_remote_copy(
            src_ref=q_ref.at[:, aligned(head_of(y, z), WIDE)],
            dst_ref=q_all.at[aligned(head, TILE)],
            send_sem=q_send.at[i],
            recv_sem=q_recv.at[i],
            device_id=at.device(y, at.core, z),
            device_id_type=MESH,
        )

    def arrive_q(i):
        y, z = at.partner(*GROUP_OFFSETS[i])
        return pltpu.make_async_remote_copy(
            src_ref=q_ref.at[:, aligned(head, WIDE)],
            dst_ref=q_all.at[aligned(head_of(y, z), TILE)],
            send_sem=q_send.at[i],
            recv_sem=q_recv.at[i],
            device_id=at.device(y, at.core, z),
            device_id_type=MESH,
        )

    def pass_on(i, source, rows_here):
        return [
            pltpu.make_async_remote_copy(
                src_ref=source[w],
                dst_ref=kv[w][1].at[rows_here],
                send_sem=pass_send.at[2 * i + w],
                recv_sem=pass_recv.at[2 * i + w],
                device_id=sibling,
                device_id_type=MESH,
            )
            for w in range(2)
        ]

    sends = []
    for i in range(len(KV_OFFSETS)):
        if i == 4:
            for j in range(3):
                sends.append(send_q(j))
                sends[-1].start()
        for copy in send_kv(i):
            copy.start()
            sends.append(copy)

    mine = [own.at[:, aligned(head, DH)] for own, _ in kv]
    last = len(KV_OFFSETS)
    for copy in pass_on(last, mine, here):
        copy.start()
        sends.append(copy)
    locals_ = [
        pltpu.make_async_copy(mine[w], kv[w][1].at[here], own_sem.at[w]) for w in range(2)
    ] + [
        pltpu.make_async_copy(
            q_ref.at[:, aligned(head, WIDE)], q_all.at[aligned(head, TILE)], own_sem.at[2]
        )
    ]
    for copy in locals_:
        copy.start()

    for i in (6, 5, 4, 0, 1, 2, 3):
        y, z = partners[i]
        came = rows_of(y, at.core, z)
        onward = pass_on(i, [whole.at[came] for _, whole in kv], came)
        for arrival, copy in zip(arrive_kv(i), onward):
            arrival.wait_recv()
            copy.start()
            sends.append(copy)

    for copy in locals_:
        copy.wait()
    for j in range(3):
        arrive_q(j).wait_recv()
    for i in range(last + 1):
        y, z = partners[i] if i < last else (at.y, at.z)
        came = rows_of(y, 1 - at.core, z)
        for copy in pass_on(i, [whole.at[came] for _, whole in kv], came):
            copy.wait_recv()
    for copy in sends:
        copy.wait_send()


def attend_kernel(
    ancestry, leaf_tiles, q_ref, k_hbm, v_hbm, out_ref,
    k_ref, v_ref, scores, peak_ref, total_ref, sum_ref, visits, sems,
):
    at = Place()
    half = at.z // 2
    k_copy = pltpu.make_async_copy(k_hbm, k_ref, sems.at[0])
    v_copy = pltpu.make_async_copy(v_hbm, v_ref, sems.at[1])
    k_copy.start()
    v_copy.start()

    tile_ids = [(2 * (j // 2) + at.core) * 4 + half * 2 + j % 2 for j in range(4)]
    homes = [leaf_tiles[a] for a in tile_ids]
    for j in range(4):
        visits[j, 0] = homes[j]

    def look(t, counts):
        after = []
        for j in range(4):
            visits[j, counts[j]] = t
            hit = jnp.logical_and(ancestry[tile_ids[j], t] == 1, t != homes[j])
            after.append(counts[j] + jnp.where(hit, 1, 0))
        return tuple(after)

    counts = lax.fori_loop(0, ancestry.shape[1], look, (jnp.int32(1),) * 4)
    for j in range(4):
        visits[j, counts[j]] = 0

    k_copy.wait()
    v_copy.wait()

    def pair_of(ref, j, i):
        first = ref[aligned(visits[j, 2 * i], TILE), :]
        second = ref[aligned(visits[j, 2 * i + 1], TILE), :]
        return jnp.concatenate([first, second], axis=0)

    for j in range(4):
        rows = pl.ds(j * TILE, TILE)
        query = jnp.concatenate(
            [q_ref[rows, pl.ds(g * DH, DH)] for g in range(GROUP)], axis=0
        )
        count = counts[j]
        steps = (count + 1) // 2

        def score(i, first):
            raw = lax.dot_general(
                query, pair_of(k_ref, j, i), (((1,), (1,)), ((), ())),
                preferred_element_type=jnp.float32,
            )
            left = raw[:, :TILE]
            if first:
                q_in = lax.broadcasted_iota(jnp.int32, (WIDE, TILE), 0) % TILE
                s_in = lax.broadcasted_iota(jnp.int32, (WIDE, TILE), 1)
                left = jnp.where(s_in <= q_in, left, NEG)
            right = raw[:, TILE:] + jnp.where(2 * i + 1 < count, 0.0, NEG)
            scores[i, :, :TILE] = left
            scores[i, :, TILE:] = right
            best = jnp.maximum(left, right)
            peak_ref[...] = best if first else jnp.maximum(peak_ref[...], best)

        score(0, True)

        @pl.loop(1, steps)
        def _(i):
            score(i, False)

        peak_ref[...] = jnp.broadcast_to(
            jnp.max(peak_ref[...], axis=1, keepdims=True), peak_ref.shape
        )

        def weigh(i, first):
            peak = peak_ref[...]
            left = jnp.exp2((scores[i, :, :TILE] - peak) * EXP2_SCALE)
            right = jnp.exp2((scores[i, :, TILE:] - peak) * EXP2_SCALE)
            rounded = jnp.concatenate(
                [left.astype(jnp.bfloat16), right.astype(jnp.bfloat16)], axis=1
            )
            update = jnp.dot(rounded, pair_of(v_ref, j, i), preferred_element_type=jnp.float32)
            both = left + right
            total_ref[...] = both if first else total_ref[...] + both
            sum_ref[...] = update if first else sum_ref[...] + update

        weigh(0, True)

        @pl.loop(1, steps)
        def _(i):
            weigh(i, False)

        result = sum_ref[...] / jnp.sum(total_ref[...], axis=1, keepdims=True)
        for g in range(GROUP):
            out_ref[rows, pl.ds(g * DH, DH)] = result[g * TILE : (g + 1) * TILE].astype(
                jnp.bfloat16
            )


def return_kernel(part_ref, out_ref, send_sem, recv_sem, own_sem):
    at = Place()
    head = head_of(at.y, at.z)
    partners = [at.partner(dy, dz) for dy, dz in GROUP_OFFSETS]
    greet([at.device(y, at.core, z) for y, z in partners])
    own = pltpu.make_async_copy(
        part_ref.at[aligned(head, TILE)], out_ref.at[:, aligned(head, WIDE)], own_sem
    )
    sends, arrivals = [], []
    for i, (y, z) in enumerate(partners):
        there = head_of(y, z)
        common = dict(
            src_ref=part_ref.at[aligned(there, TILE)],
            send_sem=send_sem.at[i],
            recv_sem=recv_sem.at[i],
            device_id=at.device(y, at.core, z),
            device_id_type=MESH,
        )
        sends.append(
            pltpu.make_async_remote_copy(dst_ref=out_ref.at[:, aligned(head, WIDE)], **common)
        )
        arrivals.append(
            pltpu.make_async_remote_copy(dst_ref=out_ref.at[:, aligned(there, WIDE)], **common)
        )
    for copy in sends:
        copy.start()
    own.start()
    own.wait()
    for copy in arrivals:
        copy.wait_recv()
    for copy in sends:
        copy.wait_send()


def on_device(group_size, queries, keys, values, ancestry, leaf_tiles):
    rows = queries.shape[0]
    total_keys = keys.shape[0] * group_size
    any_space = pl.BlockSpec(memory_space=pl.ANY)
    vmem = pl.BlockSpec(memory_space=pltpu.VMEM)
    smem = pl.BlockSpec(memory_space=pltpu.SMEM)
    dma = pltpu.SemaphoreType.DMA
    bf16 = jnp.bfloat16
    n = len(KV_OFFSETS)
    q_all, k_all, v_all = pl.pallas_call(
        gather_kernel,
        out_shape=(
            jax.ShapeDtypeStruct((4 * rows, WIDE), bf16),
            jax.ShapeDtypeStruct((total_keys, DH), bf16),
            jax.ShapeDtypeStruct((total_keys, DH), bf16),
        ),
        in_specs=[any_space] * 3,
        out_specs=[any_space] * 3,
        scratch_shapes=[
            dma((2 * n,)), dma((2 * n,)), dma((2 * n + 2,)), dma((2 * n + 2,)),
            dma((3,)), dma((3,)), dma((3,)),
        ],
        compiler_params=pltpu.CompilerParams(collective_id=0, has_side_effects=True),
        name="gather_heads",
    )(queries, keys, values)

    tiles = total_keys // TILE
    part = pl.pallas_call(
        attend_kernel,
        out_shape=jax.ShapeDtypeStruct((4 * rows, WIDE), bf16),
        in_specs=[smem, smem, vmem, any_space, any_space],
        out_specs=vmem,
        scratch_shapes=[
            pltpu.VMEM((total_keys, DH), bf16),
            pltpu.VMEM((total_keys, DH), bf16),
            pltpu.VMEM((tiles // 2, WIDE, 2 * TILE), jnp.float32),
            pltpu.VMEM((WIDE, TILE), jnp.float32),
            pltpu.VMEM((WIDE, TILE), jnp.float32),
            pltpu.VMEM((WIDE, DH), jnp.float32),
            pltpu.SMEM((4, 128), jnp.int32),
            dma((2,)),
        ],
        compiler_params=pltpu.CompilerParams(vmem_limit_bytes=48 * 1024 * 1024),
        name="attend_tree",
    )(ancestry, leaf_tiles, q_all, k_all, v_all)

    return pl.pallas_call(
        return_kernel,
        out_shape=jax.ShapeDtypeStruct((rows, KV_HEADS * WIDE), bf16),
        in_specs=[any_space],
        out_specs=any_space,
        scratch_shapes=[dma((3,)), dma((3,)), dma],
        compiler_params=pltpu.CompilerParams(collective_id=1, has_side_effects=True),
        name="return_heads",
    )(part)


def solution(mesh):
    in_specs = (
        P(("leaf", "blk", "kv"), None),
        P(("leaf", "blk", "kv"), None),
        P(("leaf", "blk", "kv"), None),
        P("leaf", None),
        P("leaf"),
    )
    out_specs = P(("leaf", "blk", "kv"), None)
    group_size = mesh.shape["blk"] * mesh.shape["kv"]
    return jax.shard_map(
        functools.partial(on_device, group_size),
        mesh=mesh, in_specs=in_specs, out_specs=out_specs, check_vma=False,
    )
```

```python
import functools
import math

import jax
import jax.numpy as jnp
from jax import lax
from jax.experimental import pallas as pl
from jax.experimental.pallas import tpu as pltpu
from jax.sharding import PartitionSpec as P

TILE = 128
KV_HEADS = 4
GROUP = 5
DH = 128
WIDE = GROUP * DH
MESH = pl.DeviceIdType.MESH
NEG = -1e30
EXP2_SCALE = math.log2(math.e) / math.sqrt(DH)

KV_OFFSETS = ((0, 3), (1, 3), (0, 2), (1, 2), (1, 1), (0, 1), (1, 0))
GROUP_OFFSETS = ((1, 1), (0, 1), (1, 0))


class Place:
    def __init__(self):
        self.leaf = lax.axis_index("leaf")
        self.blk = lax.axis_index("blk")
        self.z = lax.axis_index("kv")
        self.y = self.blk // 2
        self.core = self.blk % 2

    def partner(self, dy, dz):
        y = 1 - self.y if dy else self.y
        z = self.z
        if dz == 1:
            z = z + 1 - 2 * (z % 2)
        elif dz == 2:
            z = (z + 2) % 4
        elif dz == 3:
            z = 3 - z
        return y, z

    def device(self, y, core, z):
        return (self.leaf, 2 * y + core, z)


def head_of(y, z):
    return 2 * y + z % 2


def aligned(index, size):
    return pl.ds(pl.multiple_of(index * size, size), size)


def greet(devices):
    barrier = pltpu.get_barrier_semaphore()
    for device in devices:
        pl.semaphore_signal(barrier, inc=1, device_id=device, device_id_type=MESH)
    pl.semaphore_wait(barrier, len(devices))


def gather_kernel(
    q_ref, k_ref, v_ref, q_all, k_all, v_all,
    kv_send, kv_recv, pass_send, pass_recv, q_send, q_recv, own_sem,
):
    at = Place()
    rows = k_ref.shape[0]
    sibling = at.device(at.y, 1 - at.core, at.z)
    partners = [at.partner(dy, dz) for dy, dz in KV_OFFSETS]
    greet([at.device(y, at.core, z) for y, z in partners] + [sibling])

    head = head_of(at.y, at.z)
    here = aligned(at.blk * 4 + at.z, rows)

    def rows_of(y, core, z):
        return aligned((2 * y + core) * 4 + z, rows)

    kv = ((k_ref, k_all), (v_ref, v_all))

    def send_kv(i):
        y, z = partners[i]
        copies = []
        for w, (own, whole) in enumerate(kv):
            copies.append(
                pltpu.make_async_remote_copy(
                    src_ref=own.at[:, aligned(head_of(y, z), DH)],
                    dst_ref=whole.at[here],
                    send_sem=kv_send.at[2 * i + w],
                    recv_sem=kv_recv.at[2 * i + w],
                    device_id=at.device(y, at.core, z),
                    device_id_type=MESH,
                )
            )
        return copies

    def arrive_kv(i):
        y, z = partners[i]
        return [
            pltpu.make_async_remote_copy(
                src_ref=own.at[:, aligned(head, DH)],
                dst_ref=whole.at[rows_of(y, at.core, z)],
                send_sem=kv_send.at[2 * i + w],
                recv_sem=kv_recv.at[2 * i + w],
                device_id=at.device(y, at.core, z),
                device_id_type=MESH,
            )
            for w, (own, whole) in enumerate(kv)
        ]

    def send_q(i):
        y, z = at.partner(*GROUP_OFFSETS[i])
        return pltpu.make_async_remote_copy(
            src_ref=q_ref.at[:, aligned(head_of(y, z), WIDE)],
            dst_ref=q_all.at[aligned(head, TILE)],
            send_sem=q_send.at[i],
            recv_sem=q_recv.at[i],
            device_id=at.device(y, at.core, z),
            device_id_type=MESH,
        )

    def arrive_q(i):
        y, z = at.partner(*GROUP_OFFSETS[i])
        return pltpu.make_async_remote_copy(
            src_ref=q_ref.at[:, aligned(head, WIDE)],
            dst_ref=q_all.at[aligned(head_of(y, z), TILE)],
            send_sem=q_send.at[i],
            recv_sem=q_recv.at[i],
            device_id=at.device(y, at.core, z),
            device_id_type=MESH,
        )

    def pass_on(i, source, rows_here):
        return [
            pltpu.make_async_remote_copy(
                src_ref=source[w],
                dst_ref=kv[w][1].at[rows_here],
                send_sem=pass_send.at[2 * i + w],
                recv_sem=pass_recv.at[2 * i + w],
                device_id=sibling,
                device_id_type=MESH,
            )
            for w in range(2)
        ]

    sends = []
    for i in range(len(KV_OFFSETS)):
        if i == 4:
            for j in range(3):
                sends.append(send_q(j))
                sends[-1].start()
        for copy in send_kv(i):
            copy.start()
            sends.append(copy)

    mine = [own.at[:, aligned(head, DH)] for own, _ in kv]
    last = len(KV_OFFSETS)
    for copy in pass_on(last, mine, here):
        copy.start()
        sends.append(copy)
    locals_ = [
        pltpu.make_async_copy(mine[w], kv[w][1].at[here], own_sem.at[w]) for w in range(2)
    ] + [
        pltpu.make_async_copy(
            q_ref.at[:, aligned(head, WIDE)], q_all.at[aligned(head, TILE)], own_sem.at[2]
        )
    ]
    for copy in locals_:
        copy.start()

    for i in (6, 5, 4, 0, 1, 2, 3):
        y, z = partners[i]
        came = rows_of(y, at.core, z)
        onward = pass_on(i, [whole.at[came] for _, whole in kv], came)
        for arrival, copy in zip(arrive_kv(i), onward):
            arrival.wait_recv()
            copy.start()
            sends.append(copy)

    for copy in locals_:
        copy.wait()
    for j in range(3):
        arrive_q(j).wait_recv()
    for i in range(last + 1):
        y, z = partners[i] if i < last else (at.y, at.z)
        came = rows_of(y, 1 - at.core, z)
        for copy in pass_on(i, [whole.at[came] for _, whole in kv], came):
            copy.wait_recv()
    for copy in sends:
        copy.wait_send()


def attend_kernel(
    ancestry, leaf_tiles, q_hbm, k_hbm, v_hbm, out_ref,
    q_ref, k_ref, v_ref, scores, peak_ref, total_ref, sum_ref, visits, sems,
):
    at = Place()
    half = at.z // 2
    k_copy = pltpu.make_async_copy(k_hbm, k_ref, sems.at[0])
    v_copy = pltpu.make_async_copy(v_hbm, v_ref, sems.at[1])
    q_copy = pltpu.make_async_copy(q_hbm, q_ref, sems.at[2])
    q_copy.start()
    k_copy.start()
    v_copy.start()

    tile_ids = [(2 * (j // 2) + at.core) * 4 + half * 2 + j % 2 for j in range(4)]
    homes = [leaf_tiles[a] for a in tile_ids]
    for j in range(4):
        visits[j, 0] = homes[j]

    def look(t, counts):
        after = []
        for j in range(4):
            visits[j, counts[j]] = t
            hit = jnp.logical_and(ancestry[tile_ids[j], t] == 1, t != homes[j])
            after.append(counts[j] + jnp.where(hit, 1, 0))
        return tuple(after)

    counts = lax.fori_loop(0, ancestry.shape[1], look, (jnp.int32(1),) * 4, unroll=4)
    for j in range(4):
        visits[j, counts[j]] = 0

    q_copy.wait()
    k_copy.wait()
    v_copy.wait()

    def pair_of(ref, j, i):
        first = ref[aligned(visits[j, 2 * i], TILE), :]
        second = ref[aligned(visits[j, 2 * i + 1], TILE), :]
        return jnp.concatenate([first, second], axis=0)

    for j in range(4):
        rows = pl.ds(j * TILE, TILE)
        query = jnp.concatenate(
            [q_ref[rows, pl.ds(g * DH, DH)] for g in range(GROUP)], axis=0
        )
        count = counts[j]
        steps = (count + 1) // 2

        def score(i, first):
            raw = lax.dot_general(
                query, pair_of(k_ref, j, i), (((1,), (1,)), ((), ())),
                preferred_element_type=jnp.float32,
            )
            left = raw[:, :TILE]
            if first:
                q_in = lax.broadcasted_iota(jnp.int32, (WIDE, TILE), 0) % TILE
                s_in = lax.broadcasted_iota(jnp.int32, (WIDE, TILE), 1)
                left = jnp.where(s_in <= q_in, left, NEG)
            right = raw[:, TILE:] + jnp.where(2 * i + 1 < count, 0.0, NEG)
            scores[i, :, :TILE] = left
            scores[i, :, TILE:] = right
            best = jnp.maximum(left, right)
            peak_ref[...] = best if first else jnp.maximum(peak_ref[...], best)

        score(0, True)

        @pl.loop(1, steps)
        def _(i):
            score(i, False)

        peak_ref[...] = jnp.broadcast_to(
            jnp.max(peak_ref[...], axis=1, keepdims=True), peak_ref.shape
        )

        def weigh(i, first):
            peak = peak_ref[...]
            left = jnp.exp2((scores[i, :, :TILE] - peak) * EXP2_SCALE)
            right = jnp.exp2((scores[i, :, TILE:] - peak) * EXP2_SCALE)
            rounded = jnp.concatenate(
                [left.astype(jnp.bfloat16), right.astype(jnp.bfloat16)], axis=1
            )
            update = jnp.dot(rounded, pair_of(v_ref, j, i), preferred_element_type=jnp.float32)
            both = left + right
            total_ref[...] = both if first else total_ref[...] + both
            sum_ref[...] = update if first else sum_ref[...] + update

        weigh(0, True)

        @pl.loop(1, steps)
        def _(i):
            weigh(i, False)

        result = sum_ref[...] / jnp.sum(total_ref[...], axis=1, keepdims=True)
        for g in range(GROUP):
            out_ref[rows, pl.ds(g * DH, DH)] = result[g * TILE : (g + 1) * TILE].astype(
                jnp.bfloat16
            )


def return_kernel(part_ref, out_ref, send_sem, recv_sem, own_sem):
    at = Place()
    head = head_of(at.y, at.z)
    partners = [at.partner(dy, dz) for dy, dz in GROUP_OFFSETS]
    greet([at.device(y, at.core, z) for y, z in partners])
    own = pltpu.make_async_copy(
        part_ref.at[aligned(head, TILE)], out_ref.at[:, aligned(head, WIDE)], own_sem
    )
    sends, arrivals = [], []
    for i, (y, z) in enumerate(partners):
        there = head_of(y, z)
        common = dict(
            src_ref=part_ref.at[aligned(there, TILE)],
            send_sem=send_sem.at[i],
            recv_sem=recv_sem.at[i],
            device_id=at.device(y, at.core, z),
            device_id_type=MESH,
        )
        sends.append(
            pltpu.make_async_remote_copy(dst_ref=out_ref.at[:, aligned(head, WIDE)], **common)
        )
        arrivals.append(
            pltpu.make_async_remote_copy(dst_ref=out_ref.at[:, aligned(there, WIDE)], **common)
        )
    for copy in sends:
        copy.start()
    own.start()
    own.wait()
    for copy in arrivals:
        copy.wait_recv()
    for copy in sends:
        copy.wait_send()


def on_device(group_size, queries, keys, values, ancestry, leaf_tiles):
    rows = queries.shape[0]
    total_keys = keys.shape[0] * group_size
    any_space = pl.BlockSpec(memory_space=pl.ANY)
    vmem = pl.BlockSpec(memory_space=pltpu.VMEM)
    smem = pl.BlockSpec(memory_space=pltpu.SMEM)
    dma = pltpu.SemaphoreType.DMA
    bf16 = jnp.bfloat16
    n = len(KV_OFFSETS)
    q_all, k_all, v_all = pl.pallas_call(
        gather_kernel,
        out_shape=(
            jax.ShapeDtypeStruct((4 * rows, WIDE), bf16),
            jax.ShapeDtypeStruct((total_keys, DH), bf16),
            jax.ShapeDtypeStruct((total_keys, DH), bf16),
        ),
        in_specs=[any_space] * 3,
        out_specs=[any_space] * 3,
        scratch_shapes=[
            dma((2 * n,)), dma((2 * n,)), dma((2 * n + 2,)), dma((2 * n + 2,)),
            dma((3,)), dma((3,)), dma((3,)),
        ],
        compiler_params=pltpu.CompilerParams(
            collective_id=0, has_side_effects=True, vmem_limit_bytes=60 * 1024 * 1024
        ),
        name="gather_heads",
    )(queries, keys, values)

    tiles = total_keys // TILE
    part = pl.pallas_call(
        attend_kernel,
        out_shape=jax.ShapeDtypeStruct((4 * rows, WIDE), bf16),
        in_specs=[smem, smem, any_space, any_space, any_space],
        out_specs=vmem,
        scratch_shapes=[
            pltpu.VMEM((4 * rows, WIDE), bf16),
            pltpu.VMEM((total_keys, DH), bf16),
            pltpu.VMEM((total_keys, DH), bf16),
            pltpu.VMEM((tiles // 2, WIDE, 2 * TILE), jnp.float32),
            pltpu.VMEM((WIDE, TILE), jnp.float32),
            pltpu.VMEM((WIDE, TILE), jnp.float32),
            pltpu.VMEM((WIDE, DH), jnp.float32),
            pltpu.SMEM((4, 128), jnp.int32),
            dma((3,)),
        ],
        compiler_params=pltpu.CompilerParams(vmem_limit_bytes=60 * 1024 * 1024),
        name="attend_tree",
    )(ancestry, leaf_tiles, q_all, k_all, v_all)

    return pl.pallas_call(
        return_kernel,
        out_shape=jax.ShapeDtypeStruct((rows, KV_HEADS * WIDE), bf16),
        in_specs=[any_space],
        out_specs=any_space,
        scratch_shapes=[dma((3,)), dma((3,)), dma],
        compiler_params=pltpu.CompilerParams(
            collective_id=1, has_side_effects=True, vmem_limit_bytes=60 * 1024 * 1024
        ),
        name="return_heads",
    )(part)


def solution(mesh):
    in_specs = (
        P(("leaf", "blk", "kv"), None),
        P(("leaf", "blk", "kv"), None),
        P(("leaf", "blk", "kv"), None),
        P("leaf", None),
        P("leaf"),
    )
    out_specs = P(("leaf", "blk", "kv"), None)
    group_size = mesh.shape["blk"] * mesh.shape["kv"]
    return jax.shard_map(
        functools.partial(on_device, group_size),
        mesh=mesh, in_specs=in_specs, out_specs=out_specs, check_vma=False,
    )
```

```python
import functools
import math

import jax
import jax.numpy as jnp
from jax import lax
from jax.experimental import pallas as pl
from jax.experimental.pallas import tpu as pltpu
from jax.sharding import PartitionSpec as P

TILE = 128
KV_HEADS = 4
GROUP = 5
DH = 128
WIDE = GROUP * DH
MESH = pl.DeviceIdType.MESH
NEG = -1e30
EXP2_SCALE = math.log2(math.e) / math.sqrt(DH)

KV_OFFSETS = ((0, 3), (1, 3), (0, 2), (1, 2), (1, 1), (0, 1), (1, 0))
GROUP_OFFSETS = ((1, 1), (0, 1), (1, 0))


class Place:
    def __init__(self):
        self.leaf = lax.axis_index("leaf")
        self.blk = lax.axis_index("blk")
        self.z = lax.axis_index("kv")
        self.y = self.blk // 2
        self.core = self.blk % 2

    def partner(self, dy, dz):
        y = 1 - self.y if dy else self.y
        z = self.z
        if dz == 1:
            z = z + 1 - 2 * (z % 2)
        elif dz == 2:
            z = (z + 2) % 4
        elif dz == 3:
            z = 3 - z
        return y, z

    def device(self, y, core, z):
        return (self.leaf, 2 * y + core, z)


def head_of(y, z):
    return 2 * y + z % 2


def aligned(index, size):
    return pl.ds(pl.multiple_of(index * size, size), size)


def greet(devices):
    barrier = pltpu.get_barrier_semaphore()
    for device in devices:
        pl.semaphore_signal(barrier, inc=1, device_id=device, device_id_type=MESH)
    pl.semaphore_wait(barrier, len(devices))


def gather_kernel(
    q_ref, k_ref, v_ref, q_all, k_all, v_all,
    kv_send, kv_recv, pass_send, pass_recv, q_send, q_recv, own_sem,
):
    at = Place()
    rows = k_ref.shape[0]
    sibling = at.device(at.y, 1 - at.core, at.z)
    partners = [at.partner(dy, dz) for dy, dz in KV_OFFSETS]
    greet([at.device(y, at.core, z) for y, z in partners] + [sibling])

    head = head_of(at.y, at.z)
    here = aligned(at.blk * 4 + at.z, rows)

    def rows_of(y, core, z):
        return aligned((2 * y + core) * 4 + z, rows)

    kv = ((k_ref, k_all), (v_ref, v_all))

    def send_kv(i):
        y, z = partners[i]
        copies = []
        for w, (own, whole) in enumerate(kv):
            copies.append(
                pltpu.make_async_remote_copy(
                    src_ref=own.at[:, aligned(head_of(y, z), DH)],
                    dst_ref=whole.at[here],
                    send_sem=kv_send.at[2 * i + w],
                    recv_sem=kv_recv.at[2 * i + w],
                    device_id=at.device(y, at.core, z),
                    device_id_type=MESH,
                )
            )
        return copies

    def arrive_kv(i):
        y, z = partners[i]
        return [
            pltpu.make_async_remote_copy(
                src_ref=own.at[:, aligned(head, DH)],
                dst_ref=whole.at[rows_of(y, at.core, z)],
                send_sem=kv_send.at[2 * i + w],
                recv_sem=kv_recv.at[2 * i + w],
                device_id=at.device(y, at.core, z),
                device_id_type=MESH,
            )
            for w, (own, whole) in enumerate(kv)
        ]

    def send_q(i):
        y, z = at.partner(*GROUP_OFFSETS[i])
        return pltpu.make_async_remote_copy(
            src_ref=q_ref.at[:, aligned(head_of(y, z), WIDE)],
            dst_ref=q_all.at[aligned(head, TILE)],
            send_sem=q_send.at[i],
            recv_sem=q_recv.at[i],
            device_id=at.device(y, at.core, z),
            device_id_type=MESH,
        )

    def arrive_q(i):
        y, z = at.partner(*GROUP_OFFSETS[i])
        return pltpu.make_async_remote_copy(
            src_ref=q_ref.at[:, aligned(head, WIDE)],
            dst_ref=q_all.at[aligned(head_of(y, z), TILE)],
            send_sem=q_send.at[i],
            recv_sem=q_recv.at[i],
            device_id=at.device(y, at.core, z),
            device_id_type=MESH,
        )

    def pass_on(i, source, rows_here):
        return [
            pltpu.make_async_remote_copy(
                src_ref=source[w],
                dst_ref=kv[w][1].at[rows_here],
                send_sem=pass_send.at[2 * i + w],
                recv_sem=pass_recv.at[2 * i + w],
                device_id=sibling,
                device_id_type=MESH,
            )
            for w in range(2)
        ]

    sends = []
    for i in range(len(KV_OFFSETS)):
        if i == 4:
            for j in range(3):
                sends.append(send_q(j))
                sends[-1].start()
        for copy in send_kv(i):
            copy.start()
            sends.append(copy)

    mine = [own.at[:, aligned(head, DH)] for own, _ in kv]
    last = len(KV_OFFSETS)
    for copy in pass_on(last, mine, here):
        copy.start()
        sends.append(copy)
    locals_ = [
        pltpu.make_async_copy(mine[w], kv[w][1].at[here], own_sem.at[w]) for w in range(2)
    ] + [
        pltpu.make_async_copy(
            q_ref.at[:, aligned(head, WIDE)], q_all.at[aligned(head, TILE)], own_sem.at[2]
        )
    ]
    for copy in locals_:
        copy.start()

    for i in (6, 5, 4, 0, 1, 2, 3):
        y, z = partners[i]
        came = rows_of(y, at.core, z)
        onward = pass_on(i, [whole.at[came] for _, whole in kv], came)
        for arrival, copy in zip(arrive_kv(i), onward):
            arrival.wait_recv()
            copy.start()
            sends.append(copy)

    for copy in locals_:
        copy.wait()
    for j in range(3):
        arrive_q(j).wait_recv()
    for i in range(last + 1):
        y, z = partners[i] if i < last else (at.y, at.z)
        came = rows_of(y, 1 - at.core, z)
        for copy in pass_on(i, [whole.at[came] for _, whole in kv], came):
            copy.wait_recv()
    for copy in sends:
        copy.wait_send()


def attend_kernel(offsets, ancestry, leaf_tiles, q_ref, k_ref, v_ref, *refs):
    outs = refs[: len(offsets)]
    scores, peak_ref, total_ref, sum_ref, visits = refs[len(offsets) :]
    at = Place()
    spots = [at.partner(dy, dz) for dy, dz in offsets]
    tile_ids = [(2 * y + at.core) * 4 + z for y, z in spots]
    homes = [leaf_tiles[a] for a in tile_ids]
    tiles = range(len(offsets))
    for j in tiles:
        visits[j, 0] = homes[j]

    def look(t, counts):
        after = []
        for j in tiles:
            visits[j, counts[j]] = t
            hit = jnp.logical_and(ancestry[tile_ids[j], t] == 1, t != homes[j])
            after.append(counts[j] + jnp.where(hit, 1, 0))
        return tuple(after)

    counts = lax.fori_loop(
        0, ancestry.shape[1], look, (jnp.int32(1),) * len(offsets), unroll=8
    )
    for j in tiles:
        visits[j, counts[j]] = 0

    def pair_of(ref, j, i):
        first = ref[aligned(visits[j, 2 * i], TILE), :]
        second = ref[aligned(visits[j, 2 * i + 1], TILE), :]
        return jnp.concatenate([first, second], axis=0)

    for j in tiles:
        rows = aligned(head_of(*spots[j]), TILE)
        query = jnp.concatenate(
            [q_ref[rows, pl.ds(g * DH, DH)] for g in range(GROUP)], axis=0
        )
        count = counts[j]
        steps = (count + 1) // 2

        def score(i, first):
            raw = lax.dot_general(
                query, pair_of(k_ref, j, i), (((1,), (1,)), ((), ())),
                preferred_element_type=jnp.float32,
            )
            left = raw[:, :TILE]
            if first:
                q_in = lax.broadcasted_iota(jnp.int32, (WIDE, TILE), 0) % TILE
                s_in = lax.broadcasted_iota(jnp.int32, (WIDE, TILE), 1)
                left = jnp.where(s_in <= q_in, left, NEG)
            right = raw[:, TILE:] + jnp.where(2 * i + 1 < count, 0.0, NEG)
            scores[i, :, :TILE] = left
            scores[i, :, TILE:] = right
            best = jnp.maximum(left, right)
            peak_ref[...] = best if first else jnp.maximum(peak_ref[...], best)

        score(0, True)

        @pl.loop(1, steps)
        def _(i):
            score(i, False)

        peak_ref[...] = jnp.broadcast_to(
            jnp.max(peak_ref[...], axis=1, keepdims=True), peak_ref.shape
        )

        def weigh(i, first):
            peak = peak_ref[...]
            left = jnp.exp2((scores[i, :, :TILE] - peak) * EXP2_SCALE)
            right = jnp.exp2((scores[i, :, TILE:] - peak) * EXP2_SCALE)
            rounded = jnp.concatenate(
                [left.astype(jnp.bfloat16), right.astype(jnp.bfloat16)], axis=1
            )
            update = jnp.dot(rounded, pair_of(v_ref, j, i), preferred_element_type=jnp.float32)
            both = left + right
            total_ref[...] = both if first else total_ref[...] + both
            sum_ref[...] = update if first else sum_ref[...] + update

        weigh(0, True)

        @pl.loop(1, steps)
        def _(i):
            weigh(i, False)

        result = sum_ref[...] / jnp.sum(total_ref[...], axis=1, keepdims=True)
        for g in range(GROUP):
            outs[j][:, pl.ds(g * DH, DH)] = result[g * TILE : (g + 1) * TILE].astype(
                jnp.bfloat16
            )


def assemble_kernel(*refs):
    pieces, out_ref, sems = refs[:4], refs[4], refs[5]
    at = Place()
    copies = []
    for i, offset in enumerate(((0, 0),) + GROUP_OFFSETS):
        head = head_of(*at.partner(*offset))
        copies.append(
            pltpu.make_async_copy(
                pieces[i], out_ref.at[:, aligned(head, WIDE)], sems.at[i]
            )
        )
    for copy in copies:
        copy.start()
    for copy in copies:
        copy.wait()


def pairs_of(dy, dz):
    pairs = []
    for blk in range(4):
        for z in range(4):
            y, core = blk // 2, blk % 2
            there = z + 1 - 2 * (z % 2) if dz else z
            pairs.append((blk * 4 + z, (2 * (y ^ dy) + core) * 4 + there))
    return pairs


def on_device(group_size, queries, keys, values, ancestry, leaf_tiles):
    rows = queries.shape[0]
    total_keys = keys.shape[0] * group_size
    hbm = pl.BlockSpec(memory_space=pltpu.HBM)
    any_space = pl.BlockSpec(memory_space=pl.ANY)
    vmem = pl.BlockSpec(memory_space=pltpu.VMEM)
    smem = pl.BlockSpec(memory_space=pltpu.SMEM)
    dma = pltpu.SemaphoreType.DMA
    bf16 = jnp.bfloat16
    n = len(KV_OFFSETS)
    q_all, k_all, v_all = pl.pallas_call(
        gather_kernel,
        out_shape=(
            jax.ShapeDtypeStruct((4 * rows, WIDE), bf16),
            jax.ShapeDtypeStruct((total_keys, DH), bf16),
            jax.ShapeDtypeStruct((total_keys, DH), bf16),
        ),
        in_specs=[hbm] * 3,
        out_specs=[vmem] * 3,
        scratch_shapes=[
            dma((2 * n,)), dma((2 * n,)), dma((2 * n + 2,)), dma((2 * n + 2,)),
            dma((3,)), dma((3,)), dma((3,)),
        ],
        compiler_params=pltpu.CompilerParams(
            collective_id=0, has_side_effects=True, vmem_limit_bytes=59 * 1024 * 1024
        ),
        name="gather_heads",
    )(queries, keys, values)

    tiles = total_keys // TILE

    def attend(offsets, name):
        piece = jax.ShapeDtypeStruct((rows, WIDE), bf16)
        work = len(offsets) * 16 * WIDE * TILE * DH * 4
        return pl.pallas_call(
            functools.partial(attend_kernel, offsets),
            out_shape=(piece,) * len(offsets),
            in_specs=[smem, smem, vmem, vmem, vmem],
            out_specs=(vmem,) * len(offsets),
            scratch_shapes=[
                pltpu.VMEM((tiles // 2, WIDE, 2 * TILE), jnp.float32),
                pltpu.VMEM((WIDE, TILE), jnp.float32),
                pltpu.VMEM((WIDE, TILE), jnp.float32),
                pltpu.VMEM((WIDE, DH), jnp.float32),
                pltpu.SMEM((4, 128), jnp.int32),
            ],
            compiler_params=pltpu.CompilerParams(vmem_limit_bytes=40 * 1024 * 1024),
            cost_estimate=pl.CostEstimate(
                flops=work, bytes_accessed=4 * total_keys * DH, transcendentals=0
            ),
            name=name,
        )(ancestry, leaf_tiles, q_all, k_all, v_all)

    def send(piece, offset):
        return lax.ppermute(piece, ("blk", "kv"), pairs_of(*offset))

    far = attend(GROUP_OFFSETS[:2], "attend_far")
    arrived = [send(piece, offset) for piece, offset in zip(far, GROUP_OFFSETS)]
    (near,) = attend(GROUP_OFFSETS[2:], "attend_near")
    arrived.append(send(near, GROUP_OFFSETS[2]))
    (own,) = attend(((0, 0),), "attend_own")

    return pl.pallas_call(
        assemble_kernel,
        out_shape=jax.ShapeDtypeStruct((rows, KV_HEADS * WIDE), bf16),
        in_specs=[any_space] * 4,
        out_specs=any_space,
        scratch_shapes=[dma((4,))],
        name="assemble_heads",
    )(own, *arrived)


def solution(mesh):
    in_specs = (
        P(("leaf", "blk", "kv"), None),
        P(("leaf", "blk", "kv"), None),
        P(("leaf", "blk", "kv"), None),
        P("leaf", None),
        P("leaf"),
    )
    out_specs = P(("leaf", "blk", "kv"), None)
    group_size = mesh.shape["blk"] * mesh.shape["kv"]
    return jax.shard_map(
        functools.partial(on_device, group_size),
        mesh=mesh, in_specs=in_specs, out_specs=out_specs, check_vma=False,
    )
```

```python
import functools
import math

import jax
import jax.numpy as jnp
from jax import lax
from jax.experimental import pallas as pl
from jax.experimental.pallas import tpu as pltpu
from jax.sharding import PartitionSpec as P

TILE = 128
KV_HEADS = 4
GROUP = 5
DH = 128
WIDE = GROUP * DH
MESH = pl.DeviceIdType.MESH
NEG = -1e30
EXP2_SCALE = math.log2(math.e) / math.sqrt(DH)

KV_OFFSETS = ((0, 3), (1, 3), (0, 2), (1, 2), (1, 1), (0, 1), (1, 0))
GROUP_OFFSETS = ((1, 1), (0, 1), (1, 0))


class Place:
    def __init__(self):
        self.leaf = lax.axis_index("leaf")
        self.blk = lax.axis_index("blk")
        self.z = lax.axis_index("kv")
        self.y = self.blk // 2
        self.core = self.blk % 2

    def partner(self, dy, dz):
        y = 1 - self.y if dy else self.y
        z = self.z
        if dz == 1:
            z = z + 1 - 2 * (z % 2)
        elif dz == 2:
            z = (z + 2) % 4
        elif dz == 3:
            z = 3 - z
        return y, z

    def device(self, y, core, z):
        return (self.leaf, 2 * y + core, z)


def head_of(y, z):
    return 2 * y + z % 2


def aligned(index, size):
    return pl.ds(pl.multiple_of(index * size, size), size)


def greet(devices):
    barrier = pltpu.get_barrier_semaphore()
    for device in devices:
        pl.semaphore_signal(barrier, inc=1, device_id=device, device_id_type=MESH)
    pl.semaphore_wait(barrier, len(devices))


def gather_kernel(
    q_ref, k_ref, v_ref, q_all, k_all, v_all,
    kv_send, kv_recv, pass_send, pass_recv, q_send, q_recv, own_sem,
):
    at = Place()
    rows = k_ref.shape[0]
    sibling = at.device(at.y, 1 - at.core, at.z)
    partners = [at.partner(dy, dz) for dy, dz in KV_OFFSETS]
    greet([at.device(y, at.core, z) for y, z in partners] + [sibling])

    head = head_of(at.y, at.z)
    here = aligned(at.blk * 4 + at.z, rows)

    def rows_of(y, core, z):
        return aligned((2 * y + core) * 4 + z, rows)

    kv = ((k_ref, k_all), (v_ref, v_all))

    def send_kv(i):
        y, z = partners[i]
        copies = []
        for w, (own, whole) in enumerate(kv):
            copies.append(
                pltpu.make_async_remote_copy(
                    src_ref=own.at[:, aligned(head_of(y, z), DH)],
                    dst_ref=whole.at[here],
                    send_sem=kv_send.at[2 * i + w],
                    recv_sem=kv_recv.at[2 * i + w],
                    device_id=at.device(y, at.core, z),
                    device_id_type=MESH,
                )
            )
        return copies

    def arrive_kv(i):
        y, z = partners[i]
        return [
            pltpu.make_async_remote_copy(
                src_ref=own.at[:, aligned(head, DH)],
                dst_ref=whole.at[rows_of(y, at.core, z)],
                send_sem=kv_send.at[2 * i + w],
                recv_sem=kv_recv.at[2 * i + w],
                device_id=at.device(y, at.core, z),
                device_id_type=MESH,
            )
            for w, (own, whole) in enumerate(kv)
        ]

    def send_q(i):
        y, z = at.partner(*GROUP_OFFSETS[i])
        return pltpu.make_async_remote_copy(
            src_ref=q_ref.at[:, aligned(head_of(y, z), WIDE)],
            dst_ref=q_all.at[aligned(head, TILE)],
            send_sem=q_send.at[i],
            recv_sem=q_recv.at[i],
            device_id=at.device(y, at.core, z),
            device_id_type=MESH,
        )

    def arrive_q(i):
        y, z = at.partner(*GROUP_OFFSETS[i])
        return pltpu.make_async_remote_copy(
            src_ref=q_ref.at[:, aligned(head, WIDE)],
            dst_ref=q_all.at[aligned(head_of(y, z), TILE)],
            send_sem=q_send.at[i],
            recv_sem=q_recv.at[i],
            device_id=at.device(y, at.core, z),
            device_id_type=MESH,
        )

    def pass_on(i, source, rows_here):
        return [
            pltpu.make_async_remote_copy(
                src_ref=source[w],
                dst_ref=kv[w][1].at[rows_here],
                send_sem=pass_send.at[2 * i + w],
                recv_sem=pass_recv.at[2 * i + w],
                device_id=sibling,
                device_id_type=MESH,
            )
            for w in range(2)
        ]

    sends = []
    for i in range(len(KV_OFFSETS)):
        if i == 4:
            for j in range(3):
                sends.append(send_q(j))
                sends[-1].start()
        for copy in send_kv(i):
            copy.start()
            sends.append(copy)

    mine = [own.at[:, aligned(head, DH)] for own, _ in kv]
    last = len(KV_OFFSETS)
    for copy in pass_on(last, mine, here):
        copy.start()
        sends.append(copy)
    locals_ = [
        pltpu.make_async_copy(mine[w], kv[w][1].at[here], own_sem.at[w]) for w in range(2)
    ] + [
        pltpu.make_async_copy(
            q_ref.at[:, aligned(head, WIDE)], q_all.at[aligned(head, TILE)], own_sem.at[2]
        )
    ]
    for copy in locals_:
        copy.start()

    for i in (6, 5, 4, 0, 1, 2, 3):
        y, z = partners[i]
        came = rows_of(y, at.core, z)
        onward = pass_on(i, [whole.at[came] for _, whole in kv], came)
        for arrival, copy in zip(arrive_kv(i), onward):
            arrival.wait_recv()
            copy.start()
            sends.append(copy)

    for copy in locals_:
        copy.wait()
    for j in range(3):
        arrive_q(j).wait_recv()
    for i in range(last + 1):
        y, z = partners[i] if i < last else (at.y, at.z)
        came = rows_of(y, 1 - at.core, z)
        for copy in pass_on(i, [whole.at[came] for _, whole in kv], came):
            copy.wait_recv()
    for copy in sends:
        copy.wait_send()


def attend_kernel(offsets, ancestry, leaf_tiles, q_ref, k_ref, v_ref, *refs):
    outs = refs[: len(offsets)]
    scores, peak_ref, total_ref, sum_ref, visits = refs[len(offsets) :]
    at = Place()
    spots = [at.partner(dy, dz) for dy, dz in offsets]
    tile_ids = [(2 * y + at.core) * 4 + z for y, z in spots]
    homes = [leaf_tiles[a] for a in tile_ids]
    tiles = range(len(offsets))
    for j in tiles:
        visits[j, 0] = homes[j]

    def look(t, counts):
        after = []
        for j in tiles:
            visits[j, counts[j]] = t
            hit = jnp.logical_and(ancestry[tile_ids[j], t] == 1, t != homes[j])
            after.append(counts[j] + jnp.where(hit, 1, 0))
        return tuple(after)

    counts = lax.fori_loop(
        0, ancestry.shape[1], look, (jnp.int32(1),) * len(offsets), unroll=8
    )
    for j in tiles:
        visits[j, counts[j]] = 0

    def pair_of(ref, j, i):
        first = ref[aligned(visits[j, 2 * i], TILE), :]
        second = ref[aligned(visits[j, 2 * i + 1], TILE), :]
        return jnp.concatenate([first, second], axis=0)

    for j in tiles:
        rows = aligned(head_of(*spots[j]), TILE)
        query = jnp.concatenate(
            [q_ref[rows, pl.ds(g * DH, DH)] for g in range(GROUP)], axis=0
        )
        count = counts[j]
        steps = (count + 1) // 2

        def score(i, first):
            raw = lax.dot_general(
                query, pair_of(k_ref, j, i), (((1,), (1,)), ((), ())),
                preferred_element_type=jnp.float32,
            )
            left = raw[:, :TILE]
            if first:
                q_in = lax.broadcasted_iota(jnp.int32, (WIDE, TILE), 0) % TILE
                s_in = lax.broadcasted_iota(jnp.int32, (WIDE, TILE), 1)
                left = jnp.where(s_in <= q_in, left, NEG)
            right = raw[:, TILE:] + jnp.where(2 * i + 1 < count, 0.0, NEG)
            scores[i, :, :TILE] = left
            scores[i, :, TILE:] = right
            best = jnp.maximum(left, right)
            peak_ref[...] = best if first else jnp.maximum(peak_ref[...], best)

        score(0, True)

        @pl.loop(1, steps)
        def _(i):
            score(i, False)

        peak_ref[...] = jnp.broadcast_to(
            jnp.max(peak_ref[...], axis=1, keepdims=True), peak_ref.shape
        )

        def weigh(i, first):
            peak = peak_ref[...]
            left = jnp.exp2((scores[i, :, :TILE] - peak) * EXP2_SCALE)
            right = jnp.exp2((scores[i, :, TILE:] - peak) * EXP2_SCALE)
            rounded = jnp.concatenate(
                [left.astype(jnp.bfloat16), right.astype(jnp.bfloat16)], axis=1
            )
            update = jnp.dot(rounded, pair_of(v_ref, j, i), preferred_element_type=jnp.float32)
            both = left + right
            total_ref[...] = both if first else total_ref[...] + both
            sum_ref[...] = update if first else sum_ref[...] + update

        weigh(0, True)

        @pl.loop(1, steps)
        def _(i):
            weigh(i, False)

        result = sum_ref[...] / jnp.sum(total_ref[...], axis=1, keepdims=True)
        for g in range(GROUP):
            outs[j][:, pl.ds(g * DH, DH)] = result[g * TILE : (g + 1) * TILE].astype(
                jnp.bfloat16
            )


def assemble_kernel(*refs):
    pieces, out_ref = refs[:4], refs[4]
    at = Place()
    for i, offset in enumerate(((0, 0),) + GROUP_OFFSETS):
        head = head_of(*at.partner(*offset))
        out_ref[:, aligned(head, WIDE)] = pieces[i][...]


def pairs_of(dy, dz):
    pairs = []
    for blk in range(4):
        for z in range(4):
            y, core = blk // 2, blk % 2
            there = z + 1 - 2 * (z % 2) if dz else z
            pairs.append((blk * 4 + z, (2 * (y ^ dy) + core) * 4 + there))
    return pairs


def on_device(group_size, queries, keys, values, ancestry, leaf_tiles):
    rows = queries.shape[0]
    total_keys = keys.shape[0] * group_size
    hbm = pl.BlockSpec(memory_space=pltpu.HBM)
    vmem = pl.BlockSpec(memory_space=pltpu.VMEM)
    smem = pl.BlockSpec(memory_space=pltpu.SMEM)
    dma = pltpu.SemaphoreType.DMA
    bf16 = jnp.bfloat16
    n = len(KV_OFFSETS)
    q_all, k_all, v_all = pl.pallas_call(
        gather_kernel,
        out_shape=(
            jax.ShapeDtypeStruct((4 * rows, WIDE), bf16),
            jax.ShapeDtypeStruct((total_keys, DH), bf16),
            jax.ShapeDtypeStruct((total_keys, DH), bf16),
        ),
        in_specs=[hbm] * 3,
        out_specs=[vmem] * 3,
        scratch_shapes=[
            dma((2 * n,)), dma((2 * n,)), dma((2 * n + 2,)), dma((2 * n + 2,)),
            dma((3,)), dma((3,)), dma((3,)),
        ],
        compiler_params=pltpu.CompilerParams(
            collective_id=0, has_side_effects=True, vmem_limit_bytes=16 * 1024 * 1024
        ),
        name="gather_heads",
    )(queries, keys, values)

    tiles = total_keys // TILE

    def attend(offsets, name):
        piece = jax.ShapeDtypeStruct((rows, WIDE), bf16)
        work = len(offsets) * 16 * WIDE * TILE * DH * 4
        return pl.pallas_call(
            functools.partial(attend_kernel, offsets),
            out_shape=(piece,) * len(offsets),
            in_specs=[smem, smem, vmem, vmem, vmem],
            out_specs=(vmem,) * len(offsets),
            scratch_shapes=[
                pltpu.VMEM((tiles // 2, WIDE, 2 * TILE), jnp.float32),
                pltpu.VMEM((WIDE, TILE), jnp.float32),
                pltpu.VMEM((WIDE, TILE), jnp.float32),
                pltpu.VMEM((WIDE, DH), jnp.float32),
                pltpu.SMEM((4, 128), jnp.int32),
            ],
            compiler_params=pltpu.CompilerParams(vmem_limit_bytes=40 * 1024 * 1024),
            cost_estimate=pl.CostEstimate(
                flops=work, bytes_accessed=4 * total_keys * DH, transcendentals=0
            ),
            name=name,
        )(ancestry, leaf_tiles, q_all, k_all, v_all)

    def send(piece, offset):
        return lax.ppermute(piece, ("blk", "kv"), pairs_of(*offset))

    far = attend(GROUP_OFFSETS[:2], "attend_far")
    arrived = [send(piece, offset) for piece, offset in zip(far, GROUP_OFFSETS)]
    (near,) = attend(GROUP_OFFSETS[2:], "attend_near")
    arrived.append(send(near, GROUP_OFFSETS[2]))
    (own,) = attend(((0, 0),), "attend_own")

    return pl.pallas_call(
        assemble_kernel,
        out_shape=jax.ShapeDtypeStruct((rows, KV_HEADS * WIDE), bf16),
        in_specs=[vmem] * 4,
        out_specs=vmem,
        name="assemble_heads",
    )(own, *arrived)


def solution(mesh):
    in_specs = (
        P(("leaf", "blk", "kv"), None),
        P(("leaf", "blk", "kv"), None),
        P(("leaf", "blk", "kv"), None),
        P("leaf", None),
        P("leaf"),
    )
    out_specs = P(("leaf", "blk", "kv"), None)
    group_size = mesh.shape["blk"] * mesh.shape["kv"]
    return jax.shard_map(
        functools.partial(on_device, group_size),
        mesh=mesh, in_specs=in_specs, out_specs=out_specs, check_vma=False,
    )
```

```python
import functools
import math

import jax
import jax.numpy as jnp
from jax import lax
from jax.experimental import pallas as pl
from jax.experimental.pallas import tpu as pltpu
from jax.sharding import PartitionSpec as P

TILE = 128
KV_HEADS = 4
GROUP = 5
DH = 128
WIDE = GROUP * DH
MESH = pl.DeviceIdType.MESH
NEG = -1e30
EXP2_SCALE = math.log2(math.e) / math.sqrt(DH)

KV_OFFSETS = ((0, 3), (1, 3), (0, 2), (1, 2), (1, 1), (0, 1), (1, 0))
GROUP_OFFSETS = ((1, 1), (0, 1), (1, 0))


class Place:
    def __init__(self):
        self.leaf = lax.axis_index("leaf")
        self.blk = lax.axis_index("blk")
        self.z = lax.axis_index("kv")
        self.y = self.blk // 2
        self.core = self.blk % 2

    def partner(self, dy, dz):
        y = 1 - self.y if dy else self.y
        z = self.z
        if dz == 1:
            z = z + 1 - 2 * (z % 2)
        elif dz == 2:
            z = (z + 2) % 4
        elif dz == 3:
            z = 3 - z
        return y, z

    def device(self, y, core, z):
        return (self.leaf, 2 * y + core, z)


def head_of(y, z):
    return 2 * y + z % 2


def aligned(index, size):
    return pl.ds(pl.multiple_of(index * size, size), size)


def greet(devices):
    barrier = pltpu.get_barrier_semaphore()
    for device in devices:
        pl.semaphore_signal(barrier, inc=1, device_id=device, device_id_type=MESH)
    pl.semaphore_wait(barrier, len(devices))


def gather_kernel(
    q_ref, k_ref, v_ref, q_all, k_all, v_all,
    kv_send, kv_recv, pass_send, pass_recv, q_send, q_recv, own_sem,
):
    at = Place()
    rows = k_ref.shape[0]
    sibling = at.device(at.y, 1 - at.core, at.z)
    partners = [at.partner(dy, dz) for dy, dz in KV_OFFSETS]
    greet([at.device(y, at.core, z) for y, z in partners] + [sibling])

    head = head_of(at.y, at.z)
    here = aligned(at.blk * 4 + at.z, rows)

    def rows_of(y, core, z):
        return aligned((2 * y + core) * 4 + z, rows)

    kv = ((k_ref, k_all), (v_ref, v_all))

    def send_kv(i):
        y, z = partners[i]
        copies = []
        for w, (own, whole) in enumerate(kv):
            copies.append(
                pltpu.make_async_remote_copy(
                    src_ref=own.at[:, aligned(head_of(y, z), DH)],
                    dst_ref=whole.at[here],
                    send_sem=kv_send.at[2 * i + w],
                    recv_sem=kv_recv.at[2 * i + w],
                    device_id=at.device(y, at.core, z),
                    device_id_type=MESH,
                )
            )
        return copies

    def arrive_kv(i):
        y, z = partners[i]
        return [
            pltpu.make_async_remote_copy(
                src_ref=own.at[:, aligned(head, DH)],
                dst_ref=whole.at[rows_of(y, at.core, z)],
                send_sem=kv_send.at[2 * i + w],
                recv_sem=kv_recv.at[2 * i + w],
                device_id=at.device(y, at.core, z),
                device_id_type=MESH,
            )
            for w, (own, whole) in enumerate(kv)
        ]

    def send_q(i):
        y, z = at.partner(*GROUP_OFFSETS[i])
        return pltpu.make_async_remote_copy(
            src_ref=q_ref.at[:, aligned(head_of(y, z), WIDE)],
            dst_ref=q_all.at[aligned(head, TILE)],
            send_sem=q_send.at[i],
            recv_sem=q_recv.at[i],
            device_id=at.device(y, at.core, z),
            device_id_type=MESH,
        )

    def arrive_q(i):
        y, z = at.partner(*GROUP_OFFSETS[i])
        return pltpu.make_async_remote_copy(
            src_ref=q_ref.at[:, aligned(head, WIDE)],
            dst_ref=q_all.at[aligned(head_of(y, z), TILE)],
            send_sem=q_send.at[i],
            recv_sem=q_recv.at[i],
            device_id=at.device(y, at.core, z),
            device_id_type=MESH,
        )

    def pass_on(i, source, rows_here):
        return [
            pltpu.make_async_remote_copy(
                src_ref=source[w],
                dst_ref=kv[w][1].at[rows_here],
                send_sem=pass_send.at[2 * i + w],
                recv_sem=pass_recv.at[2 * i + w],
                device_id=sibling,
                device_id_type=MESH,
            )
            for w in range(2)
        ]

    sends = []
    for i in range(len(KV_OFFSETS)):
        if i == 4:
            for j in range(3):
                sends.append(send_q(j))
                sends[-1].start()
        for copy in send_kv(i):
            copy.start()
            sends.append(copy)

    mine = [own.at[:, aligned(head, DH)] for own, _ in kv]
    last = len(KV_OFFSETS)
    for copy in pass_on(last, mine, here):
        copy.start()
        sends.append(copy)
    locals_ = [
        pltpu.make_async_copy(mine[w], kv[w][1].at[here], own_sem.at[w]) for w in range(2)
    ] + [
        pltpu.make_async_copy(
            q_ref.at[:, aligned(head, WIDE)], q_all.at[aligned(head, TILE)], own_sem.at[2]
        )
    ]
    for copy in locals_:
        copy.start()

    for i in (6, 5, 4, 0, 1, 2, 3):
        y, z = partners[i]
        came = rows_of(y, at.core, z)
        onward = pass_on(i, [whole.at[came] for _, whole in kv], came)
        for arrival, copy in zip(arrive_kv(i), onward):
            arrival.wait_recv()
            copy.start()
            sends.append(copy)

    for copy in locals_:
        copy.wait()
    for j in range(3):
        arrive_q(j).wait_recv()
    for i in range(last + 1):
        y, z = partners[i] if i < last else (at.y, at.z)
        came = rows_of(y, 1 - at.core, z)
        for copy in pass_on(i, [whole.at[came] for _, whole in kv], came):
            copy.wait_recv()
    for copy in sends:
        copy.wait_send()


def attend_kernel(offsets, ancestry, leaf_tiles, q_hbm, k_hbm, v_hbm, *refs):
    outs = refs[: len(offsets)]
    (
        q_ref, k_ref, v_ref, scores, peak_ref, total_ref, sum_ref,
        visits, q_sems, k_sems, v_sems,
    ) = refs[len(offsets) :]
    at = Place()
    spots = [at.partner(dy, dz) for dy, dz in offsets]
    tile_ids = [(2 * y + at.core) * 4 + z for y, z in spots]
    homes = [leaf_tiles[a] for a in tile_ids]
    tiles = range(len(offsets))
    q_copies = [
        pltpu.make_async_copy(
            q_hbm.at[aligned(head_of(*spots[j]), TILE)], q_ref.at[j], q_sems.at[j]
        )
        for j in tiles
    ]
    for copy in q_copies:
        copy.start()
    for j in tiles:
        visits[j, 0] = homes[j]

    def look(t, counts):
        after = []
        for j in tiles:
            visits[j, counts[j]] = t
            hit = jnp.logical_and(ancestry[tile_ids[j], t] == 1, t != homes[j])
            after.append(counts[j] + jnp.where(hit, 1, 0))
        return tuple(after)

    counts = lax.fori_loop(
        0, ancestry.shape[1], look, (jnp.int32(1),) * len(offsets), unroll=8
    )
    for j in tiles:
        visits[j, counts[j]] = 0

    kv = ((k_hbm, k_ref, k_sems), (v_hbm, v_ref, v_sems))

    def fetch(w, j, slot):
        source, target, sems = kv[w]
        return pltpu.make_async_copy(
            source.at[aligned(visits[j, slot], TILE)],
            target.at[j, aligned(slot, TILE)],
            sems.at[j, slot],
        )

    for j in tiles:
        for w in range(2):

            @pl.loop(0, (counts[j] + 1) // 2 * 2)
            def _(slot):
                fetch(w, j, slot).start()

    def pair_of(w, j, i):
        fetch(w, j, 2 * i).wait()
        fetch(w, j, 2 * i + 1).wait()
        return kv[w][1][j, aligned(i, 2 * TILE), :]

    for j in tiles:
        q_copies[j].wait()
        query = jnp.concatenate(
            [q_ref[j, :, pl.ds(g * DH, DH)] for g in range(GROUP)], axis=0
        )
        count = counts[j]
        steps = (count + 1) // 2

        def score(i, first):
            raw = lax.dot_general(
                query, pair_of(0, j, i), (((1,), (1,)), ((), ())),
                preferred_element_type=jnp.float32,
            )
            left = raw[:, :TILE]
            if first:
                q_in = lax.broadcasted_iota(jnp.int32, (WIDE, TILE), 0) % TILE
                s_in = lax.broadcasted_iota(jnp.int32, (WIDE, TILE), 1)
                left = jnp.where(s_in <= q_in, left, NEG)
            right = raw[:, TILE:] + jnp.where(2 * i + 1 < count, 0.0, NEG)
            scores[i, :, :TILE] = left
            scores[i, :, TILE:] = right
            best = jnp.maximum(left, right)
            peak_ref[...] = best if first else jnp.maximum(peak_ref[...], best)

        score(0, True)

        @pl.loop(1, steps)
        def _(i):
            score(i, False)

        peak_ref[...] = jnp.broadcast_to(
            jnp.max(peak_ref[...], axis=1, keepdims=True), peak_ref.shape
        )

        def weigh(i, first):
            peak = peak_ref[...]
            left = jnp.exp2((scores[i, :, :TILE] - peak) * EXP2_SCALE)
            right = jnp.exp2((scores[i, :, TILE:] - peak) * EXP2_SCALE)
            rounded = jnp.concatenate(
                [left.astype(jnp.bfloat16), right.astype(jnp.bfloat16)], axis=1
            )
            update = jnp.dot(rounded, pair_of(1, j, i), preferred_element_type=jnp.float32)
            both = left + right
            total_ref[...] = both if first else total_ref[...] + both
            sum_ref[...] = update if first else sum_ref[...] + update

        weigh(0, True)

        @pl.loop(1, steps)
        def _(i):
            weigh(i, False)

        result = sum_ref[...] / jnp.sum(total_ref[...], axis=1, keepdims=True)
        for g in range(GROUP):
            outs[j][:, pl.ds(g * DH, DH)] = result[g * TILE : (g + 1) * TILE].astype(
                jnp.bfloat16
            )


def assemble_kernel(*refs):
    pieces, out_ref, sems = refs[:4], refs[4], refs[5]
    at = Place()
    copies = []
    for i, offset in enumerate(((0, 0),) + GROUP_OFFSETS):
        columns = aligned(head_of(*at.partner(*offset)), WIDE)
        copies.append(pltpu.make_async_copy(pieces[i], out_ref.at[:, columns], sems.at[i]))
    for copy in copies:
        copy.start()
    for copy in copies:
        copy.wait()


def pairs_of(dy, dz):
    pairs = []
    for blk in range(4):
        for z in range(4):
            y, core = blk // 2, blk % 2
            there = z + 1 - 2 * (z % 2) if dz else z
            pairs.append((blk * 4 + z, (2 * (y ^ dy) + core) * 4 + there))
    return pairs


def on_device(group_size, queries, keys, values, ancestry, leaf_tiles):
    rows = queries.shape[0]
    total_keys = keys.shape[0] * group_size
    any_space = pl.BlockSpec(memory_space=pl.ANY)
    vmem = pl.BlockSpec(memory_space=pltpu.VMEM)
    smem = pl.BlockSpec(memory_space=pltpu.SMEM)
    dma = pltpu.SemaphoreType.DMA
    bf16 = jnp.bfloat16
    n = len(KV_OFFSETS)
    q_all, k_all, v_all = pl.pallas_call(
        gather_kernel,
        out_shape=(
            jax.ShapeDtypeStruct((4 * rows, WIDE), bf16),
            jax.ShapeDtypeStruct((total_keys, DH), bf16),
            jax.ShapeDtypeStruct((total_keys, DH), bf16),
        ),
        in_specs=[any_space] * 3,
        out_specs=[any_space] * 3,
        scratch_shapes=[
            dma((2 * n,)), dma((2 * n,)), dma((2 * n + 2,)), dma((2 * n + 2,)),
            dma((3,)), dma((3,)), dma((3,)),
        ],
        compiler_params=pltpu.CompilerParams(
            collective_id=0, has_side_effects=True, vmem_limit_bytes=60 * 1024 * 1024
        ),
        name="gather_heads",
    )(queries, keys, values)

    tiles = total_keys // TILE

    def attend(offsets, name):
        piece = jax.ShapeDtypeStruct((rows, WIDE), bf16)
        work = len(offsets) * 16 * WIDE * TILE * DH * 4
        return pl.pallas_call(
            functools.partial(attend_kernel, offsets),
            out_shape=(piece,) * len(offsets),
            in_specs=[smem, smem, any_space, any_space, any_space],
            out_specs=(vmem,) * len(offsets),
            scratch_shapes=[
                pltpu.VMEM((len(offsets), rows, WIDE), bf16),
                pltpu.VMEM((len(offsets), total_keys, DH), bf16),
                pltpu.VMEM((len(offsets), total_keys, DH), bf16),
                pltpu.VMEM((tiles // 2, WIDE, 2 * TILE), jnp.float32),
                pltpu.VMEM((WIDE, TILE), jnp.float32),
                pltpu.VMEM((WIDE, TILE), jnp.float32),
                pltpu.VMEM((WIDE, DH), jnp.float32),
                pltpu.SMEM((4, 128), jnp.int32),
                dma((len(offsets),)),
                dma((len(offsets), tiles)),
                dma((len(offsets), tiles)),
            ],
            compiler_params=pltpu.CompilerParams(vmem_limit_bytes=60 * 1024 * 1024),
            cost_estimate=pl.CostEstimate(
                flops=work, bytes_accessed=4 * total_keys * DH, transcendentals=0
            ),
            name=name,
        )(ancestry, leaf_tiles, q_all, k_all, v_all)

    def send(piece, offset):
        return lax.ppermute(piece, ("blk", "kv"), pairs_of(*offset))

    far = attend(GROUP_OFFSETS[:2], "attend_far")
    arrived = [send(piece, offset) for piece, offset in zip(far, GROUP_OFFSETS)]
    (near,) = attend(GROUP_OFFSETS[2:], "attend_near")
    arrived.append(send(near, GROUP_OFFSETS[2]))
    (own,) = attend(((0, 0),), "attend_own")

    return pl.pallas_call(
        assemble_kernel,
        out_shape=jax.ShapeDtypeStruct((rows, KV_HEADS * WIDE), bf16),
        in_specs=[vmem] * 4,
        out_specs=any_space,
        scratch_shapes=[dma((4,))],
        name="assemble_heads",
    )(own, *arrived)


def solution(mesh):
    in_specs = (
        P(("leaf", "blk", "kv"), None),
        P(("leaf", "blk", "kv"), None),
        P(("leaf", "blk", "kv"), None),
        P("leaf", None),
        P("leaf"),
    )
    out_specs = P(("leaf", "blk", "kv"), None)
    group_size = mesh.shape["blk"] * mesh.shape["kv"]
    return jax.shard_map(
        functools.partial(on_device, group_size),
        mesh=mesh, in_specs=in_specs, out_specs=out_specs, check_vma=False,
    )
```

```python
import functools
import math

import jax
import jax.numpy as jnp
from jax import lax
from jax.experimental import pallas as pl
from jax.experimental.pallas import tpu as pltpu
from jax.sharding import PartitionSpec as P

TILE = 128
KV_HEADS = 4
GROUP = 5
DH = 128
WIDE = GROUP * DH
MESH = pl.DeviceIdType.MESH
NEG = -1e30
EXP2_SCALE = math.log2(math.e) / math.sqrt(DH)

KV_OFFSETS = ((0, 3), (1, 3), (0, 2), (1, 2), (1, 1), (0, 1), (1, 0))
GROUP_OFFSETS = ((1, 1), (0, 1), (1, 0))


class Place:
    def __init__(self):
        self.leaf = lax.axis_index("leaf")
        self.blk = lax.axis_index("blk")
        self.z = lax.axis_index("kv")
        self.y = self.blk // 2
        self.core = self.blk % 2

    def partner(self, dy, dz):
        y = 1 - self.y if dy else self.y
        z = self.z
        if dz == 1:
            z = z + 1 - 2 * (z % 2)
        elif dz == 2:
            z = (z + 2) % 4
        elif dz == 3:
            z = 3 - z
        return y, z

    def device(self, y, core, z):
        return (self.leaf, 2 * y + core, z)


def head_of(y, z):
    return 2 * y + z % 2


def aligned(index, size):
    return pl.ds(pl.multiple_of(index * size, size), size)


def greet(devices):
    barrier = pltpu.get_barrier_semaphore()
    for device in devices:
        pl.semaphore_signal(barrier, inc=1, device_id=device, device_id_type=MESH)
    pl.semaphore_wait(barrier, len(devices))


def gather_kernel(
    q_ref, k_ref, v_ref, ancestry, leaf_tiles,
    q_all, k_all, v_all, ancestry_out, leaf_tiles_out,
    kv_send, kv_recv, pass_send, pass_recv, q_send, q_recv, own_sem,
):
    at = Place()
    rows = k_ref.shape[0]
    sibling = at.device(at.y, 1 - at.core, at.z)
    partners = [at.partner(dy, dz) for dy, dz in KV_OFFSETS]
    greet([at.device(y, at.core, z) for y, z in partners] + [sibling])

    head = head_of(at.y, at.z)
    here = aligned(at.blk * 4 + at.z, rows)

    def rows_of(y, core, z):
        return aligned((2 * y + core) * 4 + z, rows)

    kv = ((k_ref, k_all), (v_ref, v_all))

    def send_kv(i):
        y, z = partners[i]
        copies = []
        for w, (own, whole) in enumerate(kv):
            copies.append(
                pltpu.make_async_remote_copy(
                    src_ref=own.at[:, aligned(head_of(y, z), DH)],
                    dst_ref=whole.at[here],
                    send_sem=kv_send.at[2 * i + w],
                    recv_sem=kv_recv.at[2 * i + w],
                    device_id=at.device(y, at.core, z),
                    device_id_type=MESH,
                )
            )
        return copies

    def arrive_kv(i):
        y, z = partners[i]
        return [
            pltpu.make_async_remote_copy(
                src_ref=own.at[:, aligned(head, DH)],
                dst_ref=whole.at[rows_of(y, at.core, z)],
                send_sem=kv_send.at[2 * i + w],
                recv_sem=kv_recv.at[2 * i + w],
                device_id=at.device(y, at.core, z),
                device_id_type=MESH,
            )
            for w, (own, whole) in enumerate(kv)
        ]

    def send_q(i):
        y, z = at.partner(*GROUP_OFFSETS[i])
        return pltpu.make_async_remote_copy(
            src_ref=q_ref.at[:, aligned(head_of(y, z), WIDE)],
            dst_ref=q_all.at[aligned(head, TILE)],
            send_sem=q_send.at[i],
            recv_sem=q_recv.at[i],
            device_id=at.device(y, at.core, z),
            device_id_type=MESH,
        )

    def arrive_q(i):
        y, z = at.partner(*GROUP_OFFSETS[i])
        return pltpu.make_async_remote_copy(
            src_ref=q_ref.at[:, aligned(head, WIDE)],
            dst_ref=q_all.at[aligned(head_of(y, z), TILE)],
            send_sem=q_send.at[i],
            recv_sem=q_recv.at[i],
            device_id=at.device(y, at.core, z),
            device_id_type=MESH,
        )

    def pass_on(i, source, rows_here):
        return [
            pltpu.make_async_remote_copy(
                src_ref=source[w],
                dst_ref=kv[w][1].at[rows_here],
                send_sem=pass_send.at[2 * i + w],
                recv_sem=pass_recv.at[2 * i + w],
                device_id=sibling,
                device_id_type=MESH,
            )
            for w in range(2)
        ]

    sends = []
    for i in range(len(KV_OFFSETS)):
        if i == 4:
            for j in range(3):
                sends.append(send_q(j))
                sends[-1].start()
        for copy in send_kv(i):
            copy.start()
            sends.append(copy)

    mine = [own.at[:, aligned(head, DH)] for own, _ in kv]
    last = len(KV_OFFSETS)
    for copy in pass_on(last, mine, here):
        copy.start()
        sends.append(copy)
    locals_ = [
        pltpu.make_async_copy(mine[w], kv[w][1].at[here], own_sem.at[w]) for w in range(2)
    ] + [
        pltpu.make_async_copy(
            q_ref.at[:, aligned(head, WIDE)], q_all.at[aligned(head, TILE)], own_sem.at[2]
        ),
        pltpu.make_async_copy(ancestry, ancestry_out, own_sem.at[3]),
        pltpu.make_async_copy(leaf_tiles, leaf_tiles_out, own_sem.at[4]),
    ]
    for copy in locals_:
        copy.start()

    for i in (6, 5, 4, 0, 1, 2, 3):
        y, z = partners[i]
        came = rows_of(y, at.core, z)
        onward = pass_on(i, [whole.at[came] for _, whole in kv], came)
        for arrival, copy in zip(arrive_kv(i), onward):
            arrival.wait_recv()
            copy.start()
            sends.append(copy)

    for copy in locals_:
        copy.wait()
    for j in range(3):
        arrive_q(j).wait_recv()
    for i in range(last + 1):
        y, z = partners[i] if i < last else (at.y, at.z)
        came = rows_of(y, 1 - at.core, z)
        for copy in pass_on(i, [whole.at[came] for _, whole in kv], came):
            copy.wait_recv()
    for copy in sends:
        copy.wait_send()


def attend_kernel(offsets, ancestry, leaf_tiles, q_ref, k_ref, v_ref, *refs):
    outs = refs[: len(offsets)]
    scores, peak_ref, total_ref, sum_ref, visits = refs[len(offsets) :]
    at = Place()
    spots = [at.partner(dy, dz) for dy, dz in offsets]
    tile_ids = [(2 * y + at.core) * 4 + z for y, z in spots]
    homes = [leaf_tiles[a] for a in tile_ids]
    tiles = range(len(offsets))
    for j in tiles:
        visits[j, 0] = homes[j]

    def look(t, counts):
        after = []
        for j in tiles:
            visits[j, counts[j]] = t
            hit = jnp.logical_and(ancestry[tile_ids[j], t] == 1, t != homes[j])
            after.append(counts[j] + jnp.where(hit, 1, 0))
        return tuple(after)

    counts = lax.fori_loop(
        0, ancestry.shape[1], look, (jnp.int32(1),) * len(offsets), unroll=8
    )
    for j in tiles:
        visits[j, counts[j]] = 0

    def pair_of(ref, j, i):
        first = ref[aligned(visits[j, 2 * i], TILE), :]
        second = ref[aligned(visits[j, 2 * i + 1], TILE), :]
        return jnp.concatenate([first, second], axis=0)

    for j in tiles:
        rows = aligned(head_of(*spots[j]), TILE)
        query = jnp.concatenate(
            [q_ref[rows, pl.ds(g * DH, DH)] for g in range(GROUP)], axis=0
        )
        count = counts[j]
        steps = (count + 1) // 2

        def score(i, first):
            raw = lax.dot_general(
                query, pair_of(k_ref, j, i), (((1,), (1,)), ((), ())),
                preferred_element_type=jnp.float32,
            )
            left = raw[:, :TILE]
            if first:
                q_in = lax.broadcasted_iota(jnp.int32, (WIDE, TILE), 0) % TILE
                s_in = lax.broadcasted_iota(jnp.int32, (WIDE, TILE), 1)
                left = jnp.where(s_in <= q_in, left, NEG)
            right = raw[:, TILE:] + jnp.where(2 * i + 1 < count, 0.0, NEG)
            scores[i, :, :TILE] = left
            scores[i, :, TILE:] = right
            best = jnp.maximum(left, right)
            peak_ref[...] = best if first else jnp.maximum(peak_ref[...], best)

        score(0, True)

        @pl.loop(1, steps)
        def _(i):
            score(i, False)

        peak_ref[...] = jnp.broadcast_to(
            jnp.max(peak_ref[...], axis=1, keepdims=True), peak_ref.shape
        )

        def weigh(i, first):
            peak = peak_ref[...]
            left = jnp.exp2((scores[i, :, :TILE] - peak) * EXP2_SCALE)
            right = jnp.exp2((scores[i, :, TILE:] - peak) * EXP2_SCALE)
            rounded = jnp.concatenate(
                [left.astype(jnp.bfloat16), right.astype(jnp.bfloat16)], axis=1
            )
            update = jnp.dot(rounded, pair_of(v_ref, j, i), preferred_element_type=jnp.float32)
            both = left + right
            total_ref[...] = both if first else total_ref[...] + both
            sum_ref[...] = update if first else sum_ref[...] + update

        weigh(0, True)

        @pl.loop(1, steps)
        def _(i):
            weigh(i, False)

        result = sum_ref[...] / jnp.sum(total_ref[...], axis=1, keepdims=True)
        for g in range(GROUP):
            outs[j][:, pl.ds(g * DH, DH)] = result[g * TILE : (g + 1) * TILE].astype(
                jnp.bfloat16
            )


def assemble_kernel(*refs):
    pieces, out_ref = refs[:4], refs[4]
    at = Place()
    for i, offset in enumerate(((0, 0),) + GROUP_OFFSETS):
        head = head_of(*at.partner(*offset))
        out_ref[:, aligned(head, WIDE)] = pieces[i][...]


def pairs_of(dy, dz):
    pairs = []
    for blk in range(4):
        for z in range(4):
            y, core = blk // 2, blk % 2
            there = z + 1 - 2 * (z % 2) if dz else z
            pairs.append((blk * 4 + z, (2 * (y ^ dy) + core) * 4 + there))
    return pairs


def on_device(group_size, queries, keys, values, ancestry, leaf_tiles):
    rows = queries.shape[0]
    total_keys = keys.shape[0] * group_size
    hbm = pl.BlockSpec(memory_space=pltpu.HBM)
    vmem = pl.BlockSpec(memory_space=pltpu.VMEM)
    smem = pl.BlockSpec(memory_space=pltpu.SMEM)
    dma = pltpu.SemaphoreType.DMA
    bf16 = jnp.bfloat16
    n = len(KV_OFFSETS)
    arguments = [
        pltpu.with_memory_space_constraint(x, pltpu.HBM)
        for x in (queries, keys, values, ancestry, leaf_tiles)
    ]
    q_all, k_all, v_all, ancestry, leaf_tiles = pl.pallas_call(
        gather_kernel,
        out_shape=(
            jax.ShapeDtypeStruct((4 * rows, WIDE), bf16),
            jax.ShapeDtypeStruct((total_keys, DH), bf16),
            jax.ShapeDtypeStruct((total_keys, DH), bf16),
            jax.ShapeDtypeStruct(ancestry.shape, ancestry.dtype),
            jax.ShapeDtypeStruct(leaf_tiles.shape, leaf_tiles.dtype),
        ),
        in_specs=[hbm] * 5,
        out_specs=[vmem] * 5,
        scratch_shapes=[
            dma((2 * n,)), dma((2 * n,)), dma((2 * n + 2,)), dma((2 * n + 2,)),
            dma((3,)), dma((3,)), dma((5,)),
        ],
        compiler_params=pltpu.CompilerParams(
            collective_id=0, has_side_effects=True, vmem_limit_bytes=16 * 1024 * 1024
        ),
        name="gather_heads",
    )(*arguments)

    tiles = total_keys // TILE

    def attend(offsets, name):
        piece = jax.ShapeDtypeStruct((rows, WIDE), bf16)
        work = len(offsets) * 16 * WIDE * TILE * DH * 4
        return pl.pallas_call(
            functools.partial(attend_kernel, offsets),
            out_shape=(piece,) * len(offsets),
            in_specs=[smem, smem, vmem, vmem, vmem],
            out_specs=(vmem,) * len(offsets),
            scratch_shapes=[
                pltpu.VMEM((tiles // 2, WIDE, 2 * TILE), jnp.float32),
                pltpu.VMEM((WIDE, TILE), jnp.float32),
                pltpu.VMEM((WIDE, TILE), jnp.float32),
                pltpu.VMEM((WIDE, DH), jnp.float32),
                pltpu.SMEM((4, 128), jnp.int32),
            ],
            compiler_params=pltpu.CompilerParams(vmem_limit_bytes=40 * 1024 * 1024),
            cost_estimate=pl.CostEstimate(
                flops=work, bytes_accessed=4 * total_keys * DH, transcendentals=0
            ),
            name=name,
        )(ancestry, leaf_tiles, q_all, k_all, v_all)

    def send(piece, offset):
        return lax.ppermute(piece, ("blk", "kv"), pairs_of(*offset))

    far = attend(GROUP_OFFSETS[:2], "attend_far")
    arrived = [send(piece, offset) for piece, offset in zip(far, GROUP_OFFSETS)]
    (near,) = attend(GROUP_OFFSETS[2:], "attend_near")
    arrived.append(send(near, GROUP_OFFSETS[2]))
    (own,) = attend(((0, 0),), "attend_own")

    return pl.pallas_call(
        assemble_kernel,
        out_shape=jax.ShapeDtypeStruct((rows, KV_HEADS * WIDE), bf16),
        in_specs=[vmem] * 4,
        out_specs=vmem,
        name="assemble_heads",
    )(own, *arrived)


def solution(mesh):
    in_specs = (
        P(("leaf", "blk", "kv"), None),
        P(("leaf", "blk", "kv"), None),
        P(("leaf", "blk", "kv"), None),
        P("leaf", None),
        P("leaf"),
    )
    out_specs = P(("leaf", "blk", "kv"), None)
    group_size = mesh.shape["blk"] * mesh.shape["kv"]
    return jax.shard_map(
        functools.partial(on_device, group_size),
        mesh=mesh, in_specs=in_specs, out_specs=out_specs, check_vma=False,
    )
```

```python
import functools
import math

import jax
import jax.numpy as jnp
from jax import lax
from jax.experimental import pallas as pl
from jax.experimental.pallas import tpu as pltpu
from jax.sharding import PartitionSpec as P

TILE = 128
KV_HEADS = 4
GROUP = 5
DH = 128
WIDE = GROUP * DH
MESH = pl.DeviceIdType.MESH
NEG = -1e30
EXP2_SCALE = math.log2(math.e) / math.sqrt(DH)

KV_OFFSETS = ((0, 3), (1, 3), (0, 2), (1, 2), (1, 1), (0, 1), (1, 0))
GROUP_OFFSETS = ((1, 1), (0, 1), (1, 0))


class Place:
    def __init__(self):
        self.leaf = lax.axis_index("leaf")
        self.blk = lax.axis_index("blk")
        self.z = lax.axis_index("kv")
        self.y = self.blk // 2
        self.core = self.blk % 2

    def partner(self, dy, dz):
        y = 1 - self.y if dy else self.y
        z = self.z
        if dz == 1:
            z = z + 1 - 2 * (z % 2)
        elif dz == 2:
            z = (z + 2) % 4
        elif dz == 3:
            z = 3 - z
        return y, z

    def device(self, y, core, z):
        return (self.leaf, 2 * y + core, z)


def head_of(y, z):
    return 2 * y + z % 2


def aligned(index, size):
    return pl.ds(pl.multiple_of(index * size, size), size)


def greet(devices):
    barrier = pltpu.get_barrier_semaphore()
    for device in devices:
        pl.semaphore_signal(barrier, inc=1, device_id=device, device_id_type=MESH)
    pl.semaphore_wait(barrier, len(devices))


def gather_kernel(
    q_ref, k_ref, v_ref, ancestry, leaf_tiles,
    q_all, k_all, v_all, ancestry_out, leaf_tiles_out,
    kv_send, kv_recv, pass_send, pass_recv, q_send, q_recv, own_sem,
):
    at = Place()
    rows = k_ref.shape[0]
    sibling = at.device(at.y, 1 - at.core, at.z)
    partners = [at.partner(dy, dz) for dy, dz in KV_OFFSETS]
    greet([at.device(y, at.core, z) for y, z in partners] + [sibling])

    head = head_of(at.y, at.z)
    here = aligned(at.blk * 4 + at.z, rows)

    def rows_of(y, core, z):
        return aligned((2 * y + core) * 4 + z, rows)

    kv = ((k_ref, k_all), (v_ref, v_all))

    def send_kv(i):
        y, z = partners[i]
        copies = []
        for w, (own, whole) in enumerate(kv):
            copies.append(
                pltpu.make_async_remote_copy(
                    src_ref=own.at[:, aligned(head_of(y, z), DH)],
                    dst_ref=whole.at[here],
                    send_sem=kv_send.at[2 * i + w],
                    recv_sem=kv_recv.at[2 * i + w],
                    device_id=at.device(y, at.core, z),
                    device_id_type=MESH,
                )
            )
        return copies

    def arrive_kv(i):
        y, z = partners[i]
        return [
            pltpu.make_async_remote_copy(
                src_ref=own.at[:, aligned(head, DH)],
                dst_ref=whole.at[rows_of(y, at.core, z)],
                send_sem=kv_send.at[2 * i + w],
                recv_sem=kv_recv.at[2 * i + w],
                device_id=at.device(y, at.core, z),
                device_id_type=MESH,
            )
            for w, (own, whole) in enumerate(kv)
        ]

    def send_q(i):
        y, z = at.partner(*GROUP_OFFSETS[i])
        return pltpu.make_async_remote_copy(
            src_ref=q_ref.at[:, aligned(head_of(y, z), WIDE)],
            dst_ref=q_all.at[aligned(head, TILE)],
            send_sem=q_send.at[i],
            recv_sem=q_recv.at[i],
            device_id=at.device(y, at.core, z),
            device_id_type=MESH,
        )

    def arrive_q(i):
        y, z = at.partner(*GROUP_OFFSETS[i])
        return pltpu.make_async_remote_copy(
            src_ref=q_ref.at[:, aligned(head, WIDE)],
            dst_ref=q_all.at[aligned(head_of(y, z), TILE)],
            send_sem=q_send.at[i],
            recv_sem=q_recv.at[i],
            device_id=at.device(y, at.core, z),
            device_id_type=MESH,
        )

    def pass_on(i, source, rows_here):
        return [
            pltpu.make_async_remote_copy(
                src_ref=source[w],
                dst_ref=kv[w][1].at[rows_here],
                send_sem=pass_send.at[2 * i + w],
                recv_sem=pass_recv.at[2 * i + w],
                device_id=sibling,
                device_id_type=MESH,
            )
            for w in range(2)
        ]

    sends = []
    for i in range(len(KV_OFFSETS)):
        if i == 4:
            for j in range(3):
                sends.append(send_q(j))
                sends[-1].start()
        for copy in send_kv(i):
            copy.start()
            sends.append(copy)

    mine = [own.at[:, aligned(head, DH)] for own, _ in kv]
    last = len(KV_OFFSETS)
    for copy in pass_on(last, mine, here):
        copy.start()
        sends.append(copy)
    locals_ = [
        pltpu.make_async_copy(mine[w], kv[w][1].at[here], own_sem.at[w]) for w in range(2)
    ] + [
        pltpu.make_async_copy(
            q_ref.at[:, aligned(head, WIDE)], q_all.at[aligned(head, TILE)], own_sem.at[2]
        ),
        pltpu.make_async_copy(ancestry, ancestry_out, own_sem.at[3]),
        pltpu.make_async_copy(leaf_tiles, leaf_tiles_out, own_sem.at[4]),
    ]
    for copy in locals_:
        copy.start()

    for i in (6, 5, 4, 0, 1, 2, 3):
        y, z = partners[i]
        came = rows_of(y, at.core, z)
        onward = pass_on(i, [whole.at[came] for _, whole in kv], came)
        for arrival, copy in zip(arrive_kv(i), onward):
            arrival.wait_recv()
            copy.start()
            sends.append(copy)

    for copy in locals_:
        copy.wait()
    for j in range(3):
        arrive_q(j).wait_recv()
    for i in range(last + 1):
        y, z = partners[i] if i < last else (at.y, at.z)
        came = rows_of(y, 1 - at.core, z)
        for copy in pass_on(i, [whole.at[came] for _, whole in kv], came):
            copy.wait_recv()
    for copy in sends:
        copy.wait_send()


def attend_kernel(offsets, ancestry, leaf_tiles, q_ref, k_ref, v_ref, *refs):
    outs = refs[: len(offsets)]
    scores, peak_ref, total_ref, sum_ref, visits = refs[len(offsets) :]
    at = Place()
    spots = [at.partner(dy, dz) for dy, dz in offsets]
    tile_ids = [(2 * y + at.core) * 4 + z for y, z in spots]
    homes = [leaf_tiles[a] for a in tile_ids]
    tiles = range(len(offsets))
    for j in tiles:
        visits[j, 0] = homes[j]

    def look(t, counts):
        after = []
        for j in tiles:
            visits[j, counts[j]] = t
            hit = jnp.logical_and(ancestry[tile_ids[j], t] == 1, t != homes[j])
            after.append(counts[j] + jnp.where(hit, 1, 0))
        return tuple(after)

    counts = lax.fori_loop(
        0, ancestry.shape[1], look, (jnp.int32(1),) * len(offsets), unroll=8
    )
    for j in tiles:
        visits[j, counts[j]] = 0

    def pair_of(ref, j, i):
        first = ref[aligned(visits[j, 2 * i], TILE), :]
        second = ref[aligned(visits[j, 2 * i + 1], TILE), :]
        return jnp.concatenate([first, second], axis=0)

    for j in tiles:
        rows = aligned(head_of(*spots[j]), TILE)
        query = jnp.concatenate(
            [q_ref[rows, pl.ds(g * DH, DH)] for g in range(GROUP)], axis=0
        )
        count = counts[j]
        steps = (count + 1) // 2

        def score(i, first):
            raw = lax.dot_general(
                query, pair_of(k_ref, j, i), (((1,), (1,)), ((), ())),
                preferred_element_type=jnp.float32,
            )
            left = raw[:, :TILE]
            if first:
                q_in = lax.broadcasted_iota(jnp.int32, (WIDE, TILE), 0) % TILE
                s_in = lax.broadcasted_iota(jnp.int32, (WIDE, TILE), 1)
                left = jnp.where(s_in <= q_in, left, NEG)
            right = raw[:, TILE:] + jnp.where(2 * i + 1 < count, 0.0, NEG)
            scores[i, :, :TILE] = left
            scores[i, :, TILE:] = right
            best = jnp.maximum(left, right)
            peak_ref[...] = best if first else jnp.maximum(peak_ref[...], best)

        score(0, True)

        @pl.loop(1, steps)
        def _(i):
            score(i, False)

        peak_ref[...] = jnp.broadcast_to(
            jnp.max(peak_ref[...], axis=1, keepdims=True), peak_ref.shape
        )

        def weigh(i, first):
            peak = peak_ref[...]
            left = jnp.exp2((scores[i, :, :TILE] - peak) * EXP2_SCALE)
            right = jnp.exp2((scores[i, :, TILE:] - peak) * EXP2_SCALE)
            rounded = jnp.concatenate(
                [left.astype(jnp.bfloat16), right.astype(jnp.bfloat16)], axis=1
            )
            update = jnp.dot(rounded, pair_of(v_ref, j, i), preferred_element_type=jnp.float32)
            both = left + right
            total_ref[...] = both if first else total_ref[...] + both
            sum_ref[...] = update if first else sum_ref[...] + update

        weigh(0, True)

        @pl.loop(1, steps)
        def _(i):
            weigh(i, False)

        result = sum_ref[...] / jnp.sum(total_ref[...], axis=1, keepdims=True)
        for g in range(GROUP):
            outs[j][:, pl.ds(g * DH, DH)] = result[g * TILE : (g + 1) * TILE].astype(
                jnp.bfloat16
            )


def assemble_kernel(*refs):
    pieces, out_ref = refs[:4], refs[4]
    at = Place()
    for i, offset in enumerate(((0, 0),) + GROUP_OFFSETS):
        head = head_of(*at.partner(*offset))
        out_ref[:, aligned(head, WIDE)] = pieces[i][...]


def pairs_of(dy, dz):
    pairs = []
    for blk in range(4):
        for z in range(4):
            y, core = blk // 2, blk % 2
            there = z + 1 - 2 * (z % 2) if dz else z
            pairs.append((blk * 4 + z, (2 * (y ^ dy) + core) * 4 + there))
    return pairs


def on_device(group_size, queries, keys, values, ancestry, leaf_tiles):
    rows = queries.shape[0]
    total_keys = keys.shape[0] * group_size
    hbm = pl.BlockSpec(memory_space=pltpu.HBM)
    vmem = pl.BlockSpec(memory_space=pltpu.VMEM)
    smem = pl.BlockSpec(memory_space=pltpu.SMEM)
    dma = pltpu.SemaphoreType.DMA
    bf16 = jnp.bfloat16
    n = len(KV_OFFSETS)
    arguments = [
        pltpu.with_memory_space_constraint(x, pltpu.HBM)
        for x in (queries, keys, values, ancestry, leaf_tiles)
    ]
    q_all, k_all, v_all, ancestry, leaf_tiles = pl.pallas_call(
        gather_kernel,
        out_shape=(
            jax.ShapeDtypeStruct((4 * rows, WIDE), bf16),
            jax.ShapeDtypeStruct((total_keys, DH), bf16),
            jax.ShapeDtypeStruct((total_keys, DH), bf16),
            jax.ShapeDtypeStruct(ancestry.shape, ancestry.dtype),
            jax.ShapeDtypeStruct(leaf_tiles.shape, leaf_tiles.dtype),
        ),
        in_specs=[hbm] * 5,
        out_specs=[vmem] * 5,
        scratch_shapes=[
            dma((2 * n,)), dma((2 * n,)), dma((2 * n + 2,)), dma((2 * n + 2,)),
            dma((3,)), dma((3,)), dma((5,)),
        ],
        compiler_params=pltpu.CompilerParams(
            collective_id=0, has_side_effects=True, vmem_limit_bytes=16 * 1024 * 1024
        ),
        name="gather_heads",
    )(*arguments)

    tiles = total_keys // TILE

    def attend(offsets, name):
        piece = jax.ShapeDtypeStruct((rows, WIDE), bf16)
        work = len(offsets) * 16 * WIDE * TILE * DH * 4
        return pl.pallas_call(
            functools.partial(attend_kernel, offsets),
            out_shape=(piece,) * len(offsets),
            in_specs=[smem, smem, vmem, vmem, vmem],
            out_specs=(vmem,) * len(offsets),
            scratch_shapes=[
                pltpu.VMEM((tiles // 2, WIDE, 2 * TILE), jnp.float32),
                pltpu.VMEM((WIDE, TILE), jnp.float32),
                pltpu.VMEM((WIDE, TILE), jnp.float32),
                pltpu.VMEM((WIDE, DH), jnp.float32),
                pltpu.SMEM((4, 128), jnp.int32),
            ],
            compiler_params=pltpu.CompilerParams(vmem_limit_bytes=40 * 1024 * 1024),
            cost_estimate=pl.CostEstimate(
                flops=work, bytes_accessed=4 * total_keys * DH, transcendentals=0
            ),
            name=name,
        )(ancestry, leaf_tiles, q_all, k_all, v_all)

    def send(piece, offset):
        return lax.ppermute(piece, ("blk", "kv"), pairs_of(*offset))

    far = attend(GROUP_OFFSETS[:2], "attend_far")
    arrived = [send(piece, offset) for piece, offset in zip(far, GROUP_OFFSETS)]
    (near,) = attend(GROUP_OFFSETS[2:], "attend_near")
    arrived.append(send(near, GROUP_OFFSETS[2]))
    (own,) = attend(((0, 0),), "attend_own")

    return pl.pallas_call(
        assemble_kernel,
        out_shape=jax.ShapeDtypeStruct((rows, KV_HEADS * WIDE), bf16),
        in_specs=[vmem] * 4,
        out_specs=vmem,
        compiler_params=pltpu.CompilerParams(vmem_limit_bytes=8 * 1024 * 1024),
        name="assemble_heads",
    )(own, *arrived)


def solution(mesh):
    in_specs = (
        P(("leaf", "blk", "kv"), None),
        P(("leaf", "blk", "kv"), None),
        P(("leaf", "blk", "kv"), None),
        P("leaf", None),
        P("leaf"),
    )
    out_specs = P(("leaf", "blk", "kv"), None)
    group_size = mesh.shape["blk"] * mesh.shape["kv"]
    return jax.shard_map(
        functools.partial(on_device, group_size),
        mesh=mesh, in_specs=in_specs, out_specs=out_specs, check_vma=False,
    )
```

```python
import functools
import math

import jax
import jax.numpy as jnp
from jax import lax
from jax.experimental import pallas as pl
from jax.experimental.pallas import tpu as pltpu
from jax.sharding import PartitionSpec as P

TILE = 128
KV_HEADS = 4
GROUP = 5
DH = 128
WIDE = GROUP * DH
MESH = pl.DeviceIdType.MESH
NEG = -1e30
EXP2_SCALE = math.log2(math.e) / math.sqrt(DH)

KV_OFFSETS = ((0, 3), (1, 3), (0, 2), (1, 2), (1, 1), (0, 1), (1, 0))
GROUP_OFFSETS = ((1, 1), (0, 1), (1, 0))


class Place:
    def __init__(self):
        self.leaf = lax.axis_index("leaf")
        self.blk = lax.axis_index("blk")
        self.z = lax.axis_index("kv")
        self.y = self.blk // 2
        self.core = self.blk % 2

    def partner(self, dy, dz):
        y = 1 - self.y if dy else self.y
        z = self.z
        if dz == 1:
            z = z + 1 - 2 * (z % 2)
        elif dz == 2:
            z = (z + 2) % 4
        elif dz == 3:
            z = 3 - z
        return y, z

    def device(self, y, core, z):
        return (self.leaf, 2 * y + core, z)


def head_of(y, z):
    return 2 * y + z % 2


def aligned(index, size):
    return pl.ds(pl.multiple_of(index * size, size), size)


def greet(devices):
    barrier = pltpu.get_barrier_semaphore()
    for device in devices:
        pl.semaphore_signal(barrier, inc=1, device_id=device, device_id_type=MESH)
    pl.semaphore_wait(barrier, len(devices))


def gather_kernel(
    q_ref, k_ref, v_ref, ancestry, leaf_tiles,
    q_all, k_all, v_all, ancestry_out, leaf_tiles_out,
    kv_send, kv_recv, pass_send, pass_recv, q_send, q_recv, own_sem,
):
    at = Place()
    rows = k_ref.shape[0]
    sibling = at.device(at.y, 1 - at.core, at.z)
    partners = [at.partner(dy, dz) for dy, dz in KV_OFFSETS]
    greet([at.device(y, at.core, z) for y, z in partners] + [sibling])

    head = head_of(at.y, at.z)
    here = aligned(at.blk * 4 + at.z, rows)

    def rows_of(y, core, z):
        return aligned((2 * y + core) * 4 + z, rows)

    kv = ((k_ref, k_all), (v_ref, v_all))

    def send_kv(i):
        y, z = partners[i]
        copies = []
        for w, (own, whole) in enumerate(kv):
            copies.append(
                pltpu.make_async_remote_copy(
                    src_ref=own.at[:, aligned(head_of(y, z), DH)],
                    dst_ref=whole.at[here],
                    send_sem=kv_send.at[2 * i + w],
                    recv_sem=kv_recv.at[2 * i + w],
                    device_id=at.device(y, at.core, z),
                    device_id_type=MESH,
                )
            )
        return copies

    def arrive_kv(i):
        y, z = partners[i]
        return [
            pltpu.make_async_remote_copy(
                src_ref=own.at[:, aligned(head, DH)],
                dst_ref=whole.at[rows_of(y, at.core, z)],
                send_sem=kv_send.at[2 * i + w],
                recv_sem=kv_recv.at[2 * i + w],
                device_id=at.device(y, at.core, z),
                device_id_type=MESH,
            )
            for w, (own, whole) in enumerate(kv)
        ]

    def send_q(i):
        y, z = at.partner(*GROUP_OFFSETS[i])
        return pltpu.make_async_remote_copy(
            src_ref=q_ref.at[:, aligned(head_of(y, z), WIDE)],
            dst_ref=q_all.at[aligned(head, TILE)],
            send_sem=q_send.at[i],
            recv_sem=q_recv.at[i],
            device_id=at.device(y, at.core, z),
            device_id_type=MESH,
        )

    def arrive_q(i):
        y, z = at.partner(*GROUP_OFFSETS[i])
        return pltpu.make_async_remote_copy(
            src_ref=q_ref.at[:, aligned(head, WIDE)],
            dst_ref=q_all.at[aligned(head_of(y, z), TILE)],
            send_sem=q_send.at[i],
            recv_sem=q_recv.at[i],
            device_id=at.device(y, at.core, z),
            device_id_type=MESH,
        )

    def pass_on(i, source, rows_here):
        return [
            pltpu.make_async_remote_copy(
                src_ref=source[w],
                dst_ref=kv[w][1].at[rows_here],
                send_sem=pass_send.at[2 * i + w],
                recv_sem=pass_recv.at[2 * i + w],
                device_id=sibling,
                device_id_type=MESH,
            )
            for w in range(2)
        ]

    sends = []
    for i in range(len(KV_OFFSETS)):
        if i == 4:
            for j in range(3):
                sends.append(send_q(j))
                sends[-1].start()
        for copy in send_kv(i):
            copy.start()
            sends.append(copy)

    mine = [own.at[:, aligned(head, DH)] for own, _ in kv]
    last = len(KV_OFFSETS)
    for copy in pass_on(last, mine, here):
        copy.start()
        sends.append(copy)
    locals_ = [
        pltpu.make_async_copy(mine[w], kv[w][1].at[here], own_sem.at[w]) for w in range(2)
    ] + [
        pltpu.make_async_copy(
            q_ref.at[:, aligned(head, WIDE)], q_all.at[aligned(head, TILE)], own_sem.at[2]
        ),
        pltpu.make_async_copy(ancestry, ancestry_out, own_sem.at[3]),
        pltpu.make_async_copy(leaf_tiles, leaf_tiles_out, own_sem.at[4]),
    ]
    for copy in locals_:
        copy.start()

    for i in (6, 5, 4, 0, 1, 2, 3):
        y, z = partners[i]
        came = rows_of(y, at.core, z)
        onward = pass_on(i, [whole.at[came] for _, whole in kv], came)
        for arrival, copy in zip(arrive_kv(i), onward):
            arrival.wait_recv()
            copy.start()
            sends.append(copy)

    for copy in locals_:
        copy.wait()
    for j in range(3):
        arrive_q(j).wait_recv()
    for i in range(last + 1):
        y, z = partners[i] if i < last else (at.y, at.z)
        came = rows_of(y, 1 - at.core, z)
        for copy in pass_on(i, [whole.at[came] for _, whole in kv], came):
            copy.wait_recv()
    for copy in sends:
        copy.wait_send()


def attend_kernel(offsets, ancestry, leaf_tiles, q_ref, k_ref, v_ref, *refs):
    outs = refs[: len(offsets)]
    scores, peak_ref, total_ref, sum_ref, visits = refs[len(offsets) :]
    at = Place()
    spots = [at.partner(dy, dz) for dy, dz in offsets]
    tile_ids = [(2 * y + at.core) * 4 + z for y, z in spots]
    homes = [leaf_tiles[a] for a in tile_ids]
    tiles = range(len(offsets))
    for j in tiles:
        visits[j, 0] = homes[j]

    def look(t, counts):
        after = []
        for j in tiles:
            visits[j, counts[j]] = t
            hit = jnp.logical_and(ancestry[tile_ids[j], t] == 1, t != homes[j])
            after.append(counts[j] + jnp.where(hit, 1, 0))
        return tuple(after)

    counts = lax.fori_loop(
        0, ancestry.shape[1], look, (jnp.int32(1),) * len(offsets), unroll=8
    )
    for j in tiles:
        visits[j, counts[j]] = 0

    def pair_of(ref, j, i):
        first = ref[aligned(visits[j, 2 * i], TILE), :]
        second = ref[aligned(visits[j, 2 * i + 1], TILE), :]
        return jnp.concatenate([first, second], axis=0)

    for j in tiles:
        rows = aligned(head_of(*spots[j]), TILE)
        queries = [q_ref[rows, pl.ds(g * DH, DH)] for g in range(GROUP)]
        parts = [pl.ds(g * TILE, TILE) for g in range(GROUP)]
        count = counts[j]
        steps = (count + 1) // 2

        def score(i, first):
            pair = pair_of(k_ref, j, i)
            for g in range(GROUP):
                raw = lax.dot_general(
                    queries[g], pair, (((1,), (1,)), ((), ())),
                    preferred_element_type=jnp.float32,
                )
                left = raw[:, :TILE]
                if first:
                    q_in = lax.broadcasted_iota(jnp.int32, (TILE, TILE), 0)
                    s_in = lax.broadcasted_iota(jnp.int32, (TILE, TILE), 1)
                    left = jnp.where(s_in <= q_in, left, NEG)
                right = raw[:, TILE:] + jnp.where(2 * i + 1 < count, 0.0, NEG)
                scores[i, parts[g], :TILE] = left
                scores[i, parts[g], TILE:] = right
                best = jnp.maximum(left, right)
                peak_ref[parts[g], :] = (
                    best if first else jnp.maximum(peak_ref[parts[g], :], best)
                )

        score(0, True)

        @pl.loop(1, steps)
        def _(i):
            score(i, False)

        peak_ref[...] = jnp.broadcast_to(
            jnp.max(peak_ref[...], axis=1, keepdims=True), peak_ref.shape
        )

        def weigh(i, first):
            pair = pair_of(v_ref, j, i)
            for g in range(GROUP):
                part = parts[g]
                peak = peak_ref[part, :]
                left = jnp.exp2((scores[i, part, :TILE] - peak) * EXP2_SCALE)
                right = jnp.exp2((scores[i, part, TILE:] - peak) * EXP2_SCALE)
                rounded = jnp.concatenate(
                    [left.astype(jnp.bfloat16), right.astype(jnp.bfloat16)], axis=1
                )
                update = jnp.dot(rounded, pair, preferred_element_type=jnp.float32)
                both = left + right
                total_ref[part, :] = both if first else total_ref[part, :] + both
                sum_ref[part, :] = update if first else sum_ref[part, :] + update

        weigh(0, True)

        @pl.loop(1, steps)
        def _(i):
            weigh(i, False)

        result = sum_ref[...] / jnp.sum(total_ref[...], axis=1, keepdims=True)
        for g in range(GROUP):
            outs[j][:, pl.ds(g * DH, DH)] = result[g * TILE : (g + 1) * TILE].astype(
                jnp.bfloat16
            )


def assemble_kernel(*refs):
    pieces, out_ref = refs[:4], refs[4]
    at = Place()
    for i, offset in enumerate(((0, 0),) + GROUP_OFFSETS):
        head = head_of(*at.partner(*offset))
        out_ref[:, aligned(head, WIDE)] = pieces[i][...]


def pairs_of(dy, dz):
    pairs = []
    for blk in range(4):
        for z in range(4):
            y, core = blk // 2, blk % 2
            there = z + 1 - 2 * (z % 2) if dz else z
            pairs.append((blk * 4 + z, (2 * (y ^ dy) + core) * 4 + there))
    return pairs


def on_device(group_size, queries, keys, values, ancestry, leaf_tiles):
    rows = queries.shape[0]
    total_keys = keys.shape[0] * group_size
    hbm = pl.BlockSpec(memory_space=pltpu.HBM)
    vmem = pl.BlockSpec(memory_space=pltpu.VMEM)
    smem = pl.BlockSpec(memory_space=pltpu.SMEM)
    dma = pltpu.SemaphoreType.DMA
    bf16 = jnp.bfloat16
    n = len(KV_OFFSETS)
    arguments = [
        pltpu.with_memory_space_constraint(x, pltpu.HBM)
        for x in (queries, keys, values, ancestry, leaf_tiles)
    ]
    q_all, k_all, v_all, ancestry, leaf_tiles = pl.pallas_call(
        gather_kernel,
        out_shape=(
            jax.ShapeDtypeStruct((4 * rows, WIDE), bf16),
            jax.ShapeDtypeStruct((total_keys, DH), bf16),
            jax.ShapeDtypeStruct((total_keys, DH), bf16),
            jax.ShapeDtypeStruct(ancestry.shape, ancestry.dtype),
            jax.ShapeDtypeStruct(leaf_tiles.shape, leaf_tiles.dtype),
        ),
        in_specs=[hbm] * 5,
        out_specs=[vmem] * 5,
        scratch_shapes=[
            dma((2 * n,)), dma((2 * n,)), dma((2 * n + 2,)), dma((2 * n + 2,)),
            dma((3,)), dma((3,)), dma((5,)),
        ],
        compiler_params=pltpu.CompilerParams(
            collective_id=0, has_side_effects=True, vmem_limit_bytes=16 * 1024 * 1024
        ),
        name="gather_heads",
    )(*arguments)

    tiles = total_keys // TILE

    def attend(offsets, name):
        piece = jax.ShapeDtypeStruct((rows, WIDE), bf16)
        work = len(offsets) * 16 * WIDE * TILE * DH * 4
        return pl.pallas_call(
            functools.partial(attend_kernel, offsets),
            out_shape=(piece,) * len(offsets),
            in_specs=[smem, smem, vmem, vmem, vmem],
            out_specs=(vmem,) * len(offsets),
            scratch_shapes=[
                pltpu.VMEM((tiles // 2, WIDE, 2 * TILE), jnp.float32),
                pltpu.VMEM((WIDE, TILE), jnp.float32),
                pltpu.VMEM((WIDE, TILE), jnp.float32),
                pltpu.VMEM((WIDE, DH), jnp.float32),
                pltpu.SMEM((4, 128), jnp.int32),
            ],
            compiler_params=pltpu.CompilerParams(vmem_limit_bytes=40 * 1024 * 1024),
            cost_estimate=pl.CostEstimate(
                flops=work, bytes_accessed=4 * total_keys * DH, transcendentals=0
            ),
            name=name,
        )(ancestry, leaf_tiles, q_all, k_all, v_all)

    def send(piece, offset):
        return lax.ppermute(piece, ("blk", "kv"), pairs_of(*offset))

    far = attend(GROUP_OFFSETS[:2], "attend_far")
    arrived = [send(piece, offset) for piece, offset in zip(far, GROUP_OFFSETS)]
    (near,) = attend(GROUP_OFFSETS[2:], "attend_near")
    arrived.append(send(near, GROUP_OFFSETS[2]))
    (own,) = attend(((0, 0),), "attend_own")

    return pl.pallas_call(
        assemble_kernel,
        out_shape=jax.ShapeDtypeStruct((rows, KV_HEADS * WIDE), bf16),
        in_specs=[vmem] * 4,
        out_specs=vmem,
        compiler_params=pltpu.CompilerParams(vmem_limit_bytes=8 * 1024 * 1024),
        name="assemble_heads",
    )(own, *arrived)


def solution(mesh):
    in_specs = (
        P(("leaf", "blk", "kv"), None),
        P(("leaf", "blk", "kv"), None),
        P(("leaf", "blk", "kv"), None),
        P("leaf", None),
        P("leaf"),
    )
    out_specs = P(("leaf", "blk", "kv"), None)
    group_size = mesh.shape["blk"] * mesh.shape["kv"]
    return jax.shard_map(
        functools.partial(on_device, group_size),
        mesh=mesh, in_specs=in_specs, out_specs=out_specs, check_vma=False,
    )
```
